128 devices in a mesh: sess: 16 (over y_hi, x, core), exp: 8 (over y_lo, z).
Axes of the slice: x: 4, y: 4 (y_hi: 2, y_lo: 2; y = y_hi * 2 + y_lo), z: 4, core: 2. Of those that a mesh axis runs over, the one named last changes fastest.
Arguments:
- residual: bfloat16 [8192, 4096], P(('sess', 'exp')), may hold values from -6 to 6
- mamba_input: bfloat16 [8192, 8192], P('sess', 'exp'), may hold values from -6 to 6
- mamba_gate: bfloat16 [8192, 8192], P('sess', 'exp'), may hold values from -6 to 6
- filter_taps: float32 [4, 8192], P(None, 'exp'), may hold values from -3 to 3
- filter_bias: float32 [8192], P('exp'), may hold values from -3 to 3
- input_select: bfloat16 [8192, 288], P('exp'), may hold values from -0.0625 to 0.0625
- step_weight: bfloat16 [256, 8192], P(None, 'exp'), may hold values from -0.375 to 0.375
- step_bias: float32 [8192], P('exp'), may hold values from -6.9 to -2.25
- decay_log: float32 [16, 8192], P(None, 'exp'), may hold values from 0 to 2.77
- skip_scale: float32 [8192], P('exp'), may hold values from 0.5 to 1.5
- output_weight: bfloat16 [8192, 4096], P('exp'), may hold values from -0.0625 to 0.0625
- query_weight: bfloat16 [4096, 4096], P(None, 'exp'), may hold values from -1 to 1
- key_matrix: bfloat16 [4096, 1024], P(None, 'exp'), may hold values from -0.09375 to 0.09375
- value_matrix: bfloat16 [4096, 1024], P(None, 'exp'), may hold values from -0.09375 to 0.09375
- head_weight: bfloat16 [4096, 4096], P('exp'), may hold values from -0.09375 to 0.09375
- cache_keys: bfloat16 [32, 256, 1024], P('sess', None, 'exp'), may hold values from -6 to 6
- stored_cache_values: bfloat16 [32, 256, 1024], P('sess', None, 'exp'), may hold values from -6 to 6
- cache_state: float32 [32, 16, 8192], P('sess', None, 'exp'), may hold values from -6 to 6
- cache_filter: bfloat16 [32, 3, 8192], P('sess', None, 'exp'), may hold values from -6 to 6
- prompt_slot: int32 [32], replicated, may hold values from 0 to 31, each once
- session_prompt: int32 [64], replicated, may hold values from 0 to 31
Outputs:
- layer_out: bfloat16 [8192, 4096], P(('sess', 'exp'))
The draws below stay inside these ranges and needn't reach their ends.
Inputs may be any that keep to these rules, and one draw needn't show every extreme that they name: `prompt_slot`: each prompt has its own row of the cache arrays. `session_prompt`: several sessions may resume from one prompt.
All inputs are finite; a program needn't handle non-finite values.
Results may differ from the reference program's by a relative error of at most 0.035.
Values may be sent and summed in bfloat16 or wider, within the bound.
No kernel may reach another device: no remote copies, remote signals or barrier semaphores. Data moves between devices by JAX's collectives and lax.ppermute only.
A program may use at most 128 MiB of HBM per device.

```python
import math
import jax
import jax.numpy as jnp
import numpy as np
from jax import lax

MODEL_WIDTH = 4096
DI = 8192
NS = 16
DTR = 256
KC = 4
HQ = 32
KEY_VALUE_HEADS = 8
HEAD_SIZE = 128
NEW = 128
CACHE_POSITIONS = 256
SESSIONS = 64
TOKENS = 8192
PROMPT_COUNT = 32
N_EXP = 8


def draw_query_weight(key, part):
    key = jax.random.fold_in(key, 11)
    random_base_key = jax.random.fold_in(key, 0)
    spread_scale = MODEL_WIDTH ** (-0.5)
    matrix = jax.random.truncated_normal(random_base_key, -6.0, 6.0, (MODEL_WIDTH, HQ * HEAD_SIZE), jnp.float32) * spread_scale
    return matrix.astype(jnp.bfloat16)


def draw_cache_keys(key, part):
    key = jax.random.fold_in(key, 23)
    random_base_key = jax.random.fold_in(key, 0)
    sampled_items = jax.random.truncated_normal(random_base_key, -6.0, 6.0, (PROMPT_COUNT, CACHE_POSITIONS, KEY_VALUE_HEADS * HEAD_SIZE), jnp.float32)
    return sampled_items.astype(jnp.bfloat16)


def plant(values, key, least, high):
    longest = values.shape.index(max(values.shape))
    spots = []
    for shift in (0, 1):
        where = [jax.random.randint(jax.random.fold_in(key, axis), (), 0, length) for axis, length in enumerate(values.shape)]
        where[longest] = (where[longest] + shift) % values.shape[longest]
        spots.append(tuple(where))
    return values.at[spots[0]].set(least).at[spots[1]].set(high)


def shard_levels(stream_key, extent, pieces, least, top_value):
    loudness, own = 1.0, jax.random.fold_in(stream_key, 6)
    for dim, shards_of in pieces:
        draws = jnp.exp(jax.random.uniform(jax.random.fold_in(own, dim), (shards_of,), jnp.float32, least / len(pieces), top_value / len(pieces)))
        loudness = loudness * jnp.repeat(draws, extent[dim] // shards_of).reshape([-1 if axis == dim else 1 for axis in range(len(extent))])
    return loudness


def cumulative_ranks(count, lean):
    portions = [(1 << 20) // math.isqrt(rank ** lean) + 1 for rank in range(1, count + 1)]
    deviation = 1 + sum(portions) // (1 << 30)
    return np.cumsum(np.array([max(1, weight // deviation) for weight in portions]))


def ranked_ids(stream_key, dims, amount, skew):
    listing = cumulative_ranks(amount, skew)
    ticket = jax.random.randint(jax.random.fold_in(stream_key, 1), dims, 0, int(listing[amount - 1]))
    standing = jnp.searchsorted(jnp.asarray(listing, jnp.int32), ticket, side="right")
    return jax.random.permutation(jax.random.fold_in(stream_key, 2), amount)[standing].astype(jnp.int32)


def normal_values(rng, shape, deviation, limit, shards=(), kind=jnp.bfloat16):
    array = deviation * jax.random.normal(rng, shape, jnp.float32)
    if shards:
        array = array * shard_levels(rng, shape, shards, -0.22, 0.18)
    return jnp.clip(array, -limit, limit).astype(kind)


def setup_inputs(seed: int = 0) -> dict:
    keys = jax.random.split(jax.random.key(seed), 22)
    return {
        "residual": normal_values(keys[0], (TOKENS, MODEL_WIDTH), 1.0, 6.0, ((0, 128),)),
        "mamba_input": normal_values(keys[1], (TOKENS, DI), 1.0, 6.0, ((0, 16), (1, 8))),
        "mamba_gate": normal_values(keys[2], (TOKENS, DI), 1.0, 6.0, ((0, 16), (1, 8))),
        "filter_taps": normal_values(keys[3], (KC, DI), KC ** -0.5, 3.0, ((1, 8),), jnp.float32),
        "filter_bias": normal_values(keys[4], (DI,), 0.5, 3.0, ((0, 8),), jnp.float32),
        "input_select": normal_values(keys[5], (DI, DTR + 2 * NS), DI ** -0.5, 0.0625, ((0, 8),)),
        "step_weight": normal_values(keys[6], (DTR, DI), DTR ** -0.5, 0.375, ((1, 8),)),
        "step_bias": jnp.clip(-6.9 + 4.65 * jax.random.uniform(keys[7], (DI,), jnp.float32) ** shard_levels(keys[7], (DI,), ((0, 8),), -0.2, 0.2), -6.9, -2.25),
        "decay_log": jnp.clip(2.77 * jax.random.uniform(keys[8], (NS, DI), jnp.float32) ** shard_levels(keys[8], (NS, DI), ((1, 8),), -0.2, 0.2), 0.0, 2.77),
        "skip_scale": jnp.clip(0.5 + 1.0 * jax.random.uniform(keys[9], (DI,), jnp.float32) ** shard_levels(keys[9], (DI,), ((0, 8),), -0.2, 0.2), 0.5, 1.5),
        "output_weight": normal_values(keys[10], (DI, MODEL_WIDTH), DI ** -0.5, 0.0625, ((0, 8),)),
        "query_weight": draw_query_weight(jax.random.fold_in(keys[21], 71), 0),
        "key_matrix": normal_values(keys[12], (MODEL_WIDTH, KEY_VALUE_HEADS * HEAD_SIZE), MODEL_WIDTH ** -0.5, 0.09375, ((1, 8),)),
        "value_matrix": normal_values(keys[13], (MODEL_WIDTH, KEY_VALUE_HEADS * HEAD_SIZE), MODEL_WIDTH ** -0.5, 0.09375, ((1, 8),)),
        "head_weight": normal_values(keys[14], (HQ * HEAD_SIZE, MODEL_WIDTH), (HQ * HEAD_SIZE) ** -0.5, 0.09375, ((0, 8),)),
        "cache_keys": draw_cache_keys(jax.random.fold_in(keys[21], 71), 0),
        "stored_cache_values": normal_values(keys[16], (PROMPT_COUNT, CACHE_POSITIONS, KEY_VALUE_HEADS * HEAD_SIZE), 1.0, 6.0, ((0, 16), (2, 8))),
        "cache_state": normal_values(keys[17], (PROMPT_COUNT, NS, DI), 1.0, 6.0, ((0, 16), (2, 8)), jnp.float32),
        "cache_filter": normal_values(keys[18], (PROMPT_COUNT, KC - 1, DI), 1.0, 6.0, ((0, 16), (2, 8))),
        "prompt_slot": jax.random.permutation(keys[19], PROMPT_COUNT).astype(jnp.int32),
        "session_prompt": plant(ranked_ids(keys[20], (SESSIONS,), PROMPT_COUNT, 2), jax.random.fold_in(keys[20], 3), 0, PROMPT_COUNT - 1).astype(jnp.int32),
    }


EPSILON = 1e-06

def grouped_product(operand, weights, groups):
    stride = operand.shape[1] // groups
    running = jnp.zeros((operand.shape[0], weights.shape[1]), jnp.float32)
    for member in range(groups):
        partial_value = jnp.dot(operand[:, member * stride:(member + 1) * stride], weights[member * stride:(member + 1) * stride], preferred_element_type=jnp.float32)
        rounded = lax.optimization_barrier(partial_value.astype(jnp.bfloat16))
        running = running + rounded.astype(jnp.float32)
    return running

def selective_scan(step_size, signal, input_mix, readout, start_state, decay_rate, unroll_by):
    sessions = start_state.shape[0]
    frames = step_size.shape[0] // sessions

    def frame_major(tensor):
        return jnp.swapaxes(tensor.reshape(sessions, frames, tensor.shape[-1]), 0, 1)

    def advance(carried, inputs):
        frame_size, frame_signal, frame_input, frame_readout = inputs
        carried = jnp.exp(frame_size[:, None, :] * decay_rate[None]) * carried + (frame_size * frame_signal)[:, None, :] * frame_input[:, :, None]
        return (carried, lax.optimization_barrier(jnp.sum(frame_readout[:, :, None] * carried, axis=1)))
    last_state, emitted = lax.scan(advance, start_state, (frame_major(step_size), frame_major(signal), frame_major(input_mix), frame_major(readout)), unroll=unroll_by)
    return jnp.swapaxes(emitted, 0, 1).reshape(sessions * frames, -1)

def attend(queries, new_keys, new_values, old_keys, old_values):
    frames = queries.shape[0]
    key_heads = new_keys.shape[1] // HEAD_SIZE
    sharing = queries.shape[1] // new_keys.shape[1]
    cached = old_keys.shape[0]
    keys_all = jnp.concatenate([old_keys, new_keys], axis=0).astype(jnp.float32).reshape(cached + frames, key_heads, HEAD_SIZE)
    values_all = jnp.concatenate([old_values, new_values], axis=0).astype(jnp.float32).reshape(cached + frames, key_heads, HEAD_SIZE)
    query_grid = queries.astype(jnp.float32).reshape(frames, key_heads, sharing, HEAD_SIZE)
    scores = jnp.einsum('qhgd,khd->hgqk', query_grid, keys_all) / math.sqrt(HEAD_SIZE)
    visible = jnp.arange(cached + frames)[None, :] <= cached + jnp.arange(frames)[:, None]
    scores = jnp.where(visible, scores, -1e+30)
    top_score = lax.optimization_barrier(jnp.max(scores, axis=-1, keepdims=True))
    lifted = jnp.exp(scores - top_score)
    weights = (lifted / lax.optimization_barrier(jnp.sum(lifted, axis=-1, keepdims=True))).astype(jnp.bfloat16)
    attended = jnp.einsum('hgqk,khd->qhgd', weights.astype(jnp.float32), values_all)
    return attended.astype(jnp.bfloat16).reshape(frames, -1)

def reference(residual, mamba_input, mamba_gate, filter_taps, filter_bias, input_select, step_weight, step_bias, decay_log, skip_scale, output_weight, query_weight, key_matrix, value_matrix, head_weight, cache_keys, stored_cache_values, cache_state, cache_filter, prompt_slot, session_prompt):
    slot_rows = prompt_slot[session_prompt]
    sessions = slot_rows.shape[0]
    channels = mamba_input.shape[1]
    tap_count = filter_taps.shape[0]
    series = jnp.concatenate([cache_filter[slot_rows].astype(jnp.float32), mamba_input.astype(jnp.float32).reshape(sessions, NEW, channels)], axis=1)
    filtered = filter_bias + sum((filter_taps[offset] * series[:, offset:offset + NEW] for offset in range(tap_count)))
    filter_out = jax.nn.silu(filtered).astype(jnp.bfloat16).reshape(sessions * NEW, channels)
    projected = jnp.dot(filter_out, input_select, preferred_element_type=jnp.float32)
    step_rank = step_weight.shape[0]
    states = decay_log.shape[0]
    step_in = projected[:, :step_rank].astype(jnp.bfloat16)
    step_size = jax.nn.softplus(jnp.dot(step_in, step_weight, preferred_element_type=jnp.float32) + step_bias)
    input_mix = projected[:, step_rank:step_rank + states]
    readout = projected[:, step_rank + states:]
    signal = filter_out.astype(jnp.float32)
    emitted = selective_scan(step_size, signal, input_mix, readout, cache_state[slot_rows], -jnp.exp(decay_log), 1)
    gated = ((emitted + skip_scale * signal) * jax.nn.silu(mamba_gate.astype(jnp.float32))).astype(jnp.bfloat16)
    after_mamba = residual.astype(jnp.float32) + grouped_product(gated, output_weight, N_EXP)
    normed = (after_mamba * lax.rsqrt(lax.optimization_barrier(jnp.mean(after_mamba * after_mamba, axis=-1, keepdims=True)) + EPSILON)).astype(jnp.bfloat16)
    queries = jnp.dot(normed, query_weight, preferred_element_type=jnp.float32).astype(jnp.bfloat16)
    new_keys = jnp.dot(normed, key_matrix, preferred_element_type=jnp.float32).astype(jnp.bfloat16)
    new_values = jnp.dot(normed, value_matrix, preferred_element_type=jnp.float32).astype(jnp.bfloat16)

    def one_session(inputs):
        session_queries, session_keys, session_values, session_slot = inputs
        return attend(session_queries, session_keys, session_values, cache_keys[session_slot], stored_cache_values[session_slot])
    heads_out = lax.map(one_session, (queries.reshape(sessions, NEW, -1), new_keys.reshape(sessions, NEW, -1), new_values.reshape(sessions, NEW, -1), slot_rows))
    head_total = grouped_product(heads_out.reshape(sessions * NEW, -1), head_weight, N_EXP)
    return (after_mamba + head_total).astype(jnp.bfloat16)
```

```python
import functools
import math

import jax
import jax.numpy as jnp
from jax import lax
from jax.experimental import pallas as pl
from jax.experimental.pallas import tpu as pltpu
from jax.sharding import PartitionSpec as P

HEAD_SIZE = 128
NEW = 128
OWN = 64
EPSILON = 1e-06
LOG2E = math.log2(math.e)
MIB = 1 << 20


def y_swap():
    return [(y * 4 + z, (1 - y) * 4 + z) for y in range(2) for z in range(4)]


def z_shift(d):
    return [(y * 4 + z, y * 4 + (z + d) % 4) for y in range(2) for z in range(4)]


def sess_shift(far, x, core):
    return [
        (f * 8 + a * 2 + c, (f ^ far) * 8 + ((a + x) % 4) * 2 + (c ^ core))
        for f in range(2)
        for a in range(4)
        for c in range(2)
    ]


def sess_gather(value):
    pair = jnp.concatenate([value, lax.ppermute(value, "sess", sess_shift(1, 0, 0))], axis=0)
    mine = jnp.concatenate(
        [pair] + [lax.ppermute(pair, "sess", sess_shift(0, -d, 0)) for d in (1, 2, 3)], axis=0
    )
    return mine, lax.ppermute(mine, "sess", sess_shift(0, 0, 1))


def exp_gather(value):
    pair = jnp.stack([value, lax.ppermute(value, "exp", y_swap())])
    return jnp.stack([pair] + [lax.ppermute(pair, "exp", z_shift(-d)) for d in (1, 2, 3)])


def session_of(g, meta):
    return ((meta[1] >> 2) ^ (1 - (g >> 1))) * 2 + (g & 1)


def place_of(g, meta, prompts, slots):
    slot = slots[prompts[meta[0] * 4 + session_of(g, meta)]]
    holder = slot >> 1
    far = (holder >> 3) ^ (meta[0] >> 3)
    x = ((holder >> 1) - (meta[0] >> 1)) & 3
    return (x * 2 + far) * 2 + (slot & 1), (holder ^ meta[0]) & 1


def z_step(g, half, meta):
    return ((g & 1) * 2 + half - meta[1]) & 3


def row_of(g, meta, prompts, slots):
    return place_of(g, meta, prompts, slots)[0]


def side_of(g, meta, prompts, slots):
    return place_of(g, meta, prompts, slots)[1]


def conv_kernel(
    meta, prompts, slots, x_ref, here_ref, there_ref, taps_ref, bias_ref, select_ref, out_ref, part_ref, series
):
    g = pl.program_id(0)
    new, channels = x_ref.shape
    rows = here_ref.shape[1]
    here = here_ref[0].astype(jnp.float32)
    there = there_ref[0].astype(jnp.float32)
    series[8 - rows : 8] = jnp.where(side_of(g, meta, prompts, slots) == 1, there, here)
    series[8:] = x_ref[...].astype(jnp.float32)
    total = jnp.broadcast_to(bias_ref[...], (new, channels))
    for k in range(taps_ref.shape[0]):
        total += taps_ref[k : k + 1] * series[8 - rows + k : 8 - rows + k + new]
    out = (total / (1.0 + jnp.exp(-total))).astype(jnp.bfloat16)
    out_ref[...] = out
    part_ref[...] = jnp.dot(
        out, select_ref[...], preferred_element_type=jnp.float32
    ).astype(jnp.bfloat16)


def whole(a):
    return pl.BlockSpec(a.shape, lambda *_: (0,) * a.ndim)


def conv_project(scalars, x, here, there, taps, bias, select):
    tokens, channels = x.shape
    rows = here.shape[1]
    bias = bias.reshape(1, channels)

    def by_session(g, meta, prompts, slots):
        return session_of(g, meta), 0

    def by_row(g, *refs):
        return row_of(g, *refs), 0, 0

    return pl.pallas_call(
        conv_kernel,
        grid_spec=pltpu.PrefetchScalarGridSpec(
            num_scalar_prefetch=3,
            grid=(tokens // NEW,),
            in_specs=[
                pl.BlockSpec((NEW, channels), by_session),
                pl.BlockSpec((1, rows, channels), by_row),
                pl.BlockSpec((1, rows, channels), by_row),
                whole(taps),
                whole(bias),
                whole(select),
            ],
            out_specs=[
                pl.BlockSpec((NEW, channels), by_session),
                pl.BlockSpec((NEW, select.shape[1]), by_session),
            ],
            scratch_shapes=[pltpu.VMEM((NEW + 8, channels), jnp.float32)],
        ),
        out_shape=[
            jax.ShapeDtypeStruct((tokens, channels), jnp.bfloat16),
            jax.ShapeDtypeStruct((tokens, select.shape[1]), jnp.bfloat16),
        ],
        compiler_params=pltpu.CompilerParams(vmem_limit_bytes=32 * MIB),
        name="conv_project",
    )(*scalars, x, here, there, taps, bias, select)


def scan_kernel(
    meta,
    prompts,
    slots,
    first_ref,
    second_ref,
    signal_ref,
    gate_ref,
    weight_ref,
    bias_ref,
    decay_ref,
    here_ref,
    there_ref,
    skip_ref,
    gated_ref,
    rate_s,
    state_s,
    step_s,
    drive_s,
    emit_s,
    mix_s,
):
    g = pl.program_id(0)
    new, channels = signal_ref.shape
    states = decay_ref.shape[0]
    blocks = channels // 128
    rank = weight_ref.shape[0]
    half = new // 2

    @pl.when(g == 0)
    def _():
        rate = jnp.exp(decay_ref[...]) * (-LOG2E)
        for b in range(blocks):
            rate_s[:, b, :] = rate[:, b * 128 : (b + 1) * 128]

    start = jnp.where(
        side_of(g, meta, prompts, slots) == 1,
        there_ref[0].astype(jnp.float32),
        here_ref[0].astype(jnp.float32),
    )
    for b in range(blocks):
        state_s[:, b, :] = start[:, b * 128 : (b + 1) * 128]
    projected = jnp.concatenate([first_ref[0, 0], second_ref[0, 0]], axis=0)
    before = (
        jnp.dot(projected[:, :rank], weight_ref[...], preferred_element_type=jnp.float32)
        + bias_ref[...]
    )
    size = jnp.maximum(before, 0.0) + jnp.log1p(jnp.exp(-jnp.abs(before)))
    drive = size * signal_ref[...].astype(jnp.float32)
    for b in range(blocks):
        cols = slice(b * 128, (b + 1) * 128)
        step_s[:, b] = size[:, cols].reshape(new // 8, 8, 128)
        drive_s[:, b] = drive[:, cols].reshape(new // 8, 8, 128)
    mix = jnp.transpose(projected[:, rank:].astype(jnp.float32))
    for t in range(new):
        mix_s[t] = jnp.broadcast_to(mix[:, t : t + 1], (2 * states, 128))

    def advance(i, state):
        state = list(state)
        for s in range(8):
            d = step_s[i, :, s, :]
            u = drive_s[i, :, s, :]
            t = i * 8 + s
            total = None
            for n in range(states):
                state[n] = jnp.exp2(d * rate_s[n]) * state[n] + u * mix_s[t, n : n + 1, :]
                term = state[n] * mix_s[t, states + n : states + n + 1, :]
                total = term if total is None else total + term
            emit_s[i, :, s, :] = total
        return tuple(state)

    lax.fori_loop(0, new // 8, advance, tuple(state_s[n] for n in range(states)))
    for b in range(blocks):
        cols = slice(b * 128, (b + 1) * 128)
        emitted = emit_s[:, b].reshape(new, 128)
        gate = gate_ref[:, cols].astype(jnp.float32)
        signal = signal_ref[:, cols].astype(jnp.float32)
        gated = (
            (emitted + skip_ref[:, cols] * signal) * (gate / (1.0 + jnp.exp(-gate)))
        ).astype(jnp.bfloat16)
        for k in range(2):
            gated_ref[0, z_step(g, k, meta), :, cols] = gated[k * half : (k + 1) * half]


def scan_gate(scalars, projected, signal, gate, weight, bias, decay, here, there, skip):
    tokens, channels = signal.shape
    states = decay.shape[0]
    blocks = channels // 128
    width = projected.shape[-1]
    bias = bias.reshape(1, channels)
    skip = skip.reshape(1, channels)

    def by_session(g, meta, prompts, slots):
        return session_of(g, meta), 0

    def by_row(g, *refs):
        return row_of(g, *refs), 0, 0

    def piece(half):
        return lambda g, meta, prompts, slots: (z_step(g, half, meta), 1 - (g >> 1), 0, 0)

    return pl.pallas_call(
        scan_kernel,
        grid_spec=pltpu.PrefetchScalarGridSpec(
            num_scalar_prefetch=3,
            grid=(tokens // NEW,),
            in_specs=[
                pl.BlockSpec((1, 1, OWN, width), piece(0)),
                pl.BlockSpec((1, 1, OWN, width), piece(1)),
                pl.BlockSpec((NEW, channels), by_session),
                pl.BlockSpec((NEW, channels), by_session),
                whole(weight),
                whole(bias),
                whole(decay),
                pl.BlockSpec((1, states, channels), by_row),
                pl.BlockSpec((1, states, channels), by_row),
                whole(skip),
            ],
            out_specs=pl.BlockSpec(
                (1, 4, OWN, channels), lambda g, *_: (1 - (g >> 1), 0, 0, 0)
            ),
            scratch_shapes=[
                pltpu.VMEM((states, blocks, 128), jnp.float32),
                pltpu.VMEM((states, blocks, 128), jnp.float32),
                pltpu.VMEM((NEW // 8, blocks, 8, 128), jnp.float32),
                pltpu.VMEM((NEW // 8, blocks, 8, 128), jnp.float32),
                pltpu.VMEM((NEW // 8, blocks, 8, 128), jnp.float32),
                pltpu.VMEM((NEW, 2 * states, 128), jnp.float32),
            ],
        ),
        out_shape=jax.ShapeDtypeStruct((2, 4, OWN, channels), jnp.bfloat16),
        compiler_params=pltpu.CompilerParams(vmem_limit_bytes=32 * MIB),
        name="scan_gate",
    )(*scalars, projected, projected, signal, gate, weight, bias, decay, here, there, skip)


def attend_kernel(
    meta, prompts, slots, *refs
):
    (*rows_refs, here_k, here_v, there_k, there_v, out_ref) = refs
    g = pl.program_id(0)
    rows = jnp.concatenate([r[0, 0, 0] for r in rows_refs], axis=0)
    there = side_of(g, meta, prompts, slots) == 1
    old_keys = jnp.where(there, there_k[0], here_k[0])
    old_values = jnp.where(there, there_v[0], here_v[0])
    new = rows.shape[0]
    heads = rows.shape[1] // HEAD_SIZE - 2
    new_keys = rows[:, heads * HEAD_SIZE : (heads + 1) * HEAD_SIZE]
    new_values = rows[:, (heads + 1) * HEAD_SIZE :]
    queries = jnp.concatenate(
        [rows[:, k * HEAD_SIZE : (k + 1) * HEAD_SIZE] for k in range(heads)], axis=0
    )
    contract = (((1,), (1,)), ((), ()))
    scale = 1.0 / math.sqrt(HEAD_SIZE)
    old = lax.dot_general(queries, old_keys, contract, preferred_element_type=jnp.float32) * scale
    fresh = lax.dot_general(queries, new_keys, contract, preferred_element_type=jnp.float32) * scale
    at = lax.broadcasted_iota(jnp.int32, fresh.shape, 0) & (new - 1)
    fresh = jnp.where(lax.broadcasted_iota(jnp.int32, fresh.shape, 1) <= at, fresh, -1e30)
    top = jnp.maximum(
        jnp.max(old, axis=-1, keepdims=True), jnp.max(fresh, axis=-1, keepdims=True)
    )
    old = jnp.exp(old - top)
    fresh = jnp.exp(fresh - top)
    total = jnp.sum(old, axis=-1, keepdims=True) + jnp.sum(fresh, axis=-1, keepdims=True)
    inverse = 1.0 / total
    attended = jnp.dot(
        (old * inverse).astype(jnp.bfloat16), old_values, preferred_element_type=jnp.float32
    ) + jnp.dot(
        (fresh * inverse).astype(jnp.bfloat16), new_values, preferred_element_type=jnp.float32
    )
    attended = attended.astype(jnp.bfloat16)
    half = new // 2
    for k in range(2):
        for n in range(heads):
            out_ref[0, z_step(g, k, meta), :, n * HEAD_SIZE : (n + 1) * HEAD_SIZE] = attended[
                n * new + k * half : n * new + (k + 1) * half
            ]


def attend(scalars, rows, here_k, here_v, there_k, there_v):
    width = rows.shape[-1]
    quarter = rows.shape[3]
    cached = here_k.shape[1]
    query_width = width - 2 * HEAD_SIZE

    def piece(half, part):
        return lambda g, meta, prompts, slots: (part, 1 - (g >> 1), z_step(g, half, meta), 0, 0)

    def by_row(g, *refs):
        return row_of(g, *refs), 0, 0

    old = pl.BlockSpec((1, cached, HEAD_SIZE), by_row)
    return pl.pallas_call(
        attend_kernel,
        grid_spec=pltpu.PrefetchScalarGridSpec(
            num_scalar_prefetch=3,
            grid=(4,),
            in_specs=[
                pl.BlockSpec((1, 1, 1, quarter, width), piece(half, part))
                for half in range(2)
                for part in range(2)
            ]
            + [old] * 4,
            out_specs=pl.BlockSpec(
                (1, 4, OWN, query_width), lambda g, *_: (1 - (g >> 1), 0, 0, 0)
            ),
        ),
        out_shape=jax.ShapeDtypeStruct((2, 4, OWN, query_width), jnp.bfloat16),
        compiler_params=pltpu.CompilerParams(vmem_limit_bytes=32 * MIB),
        name="attend",
    )(*scalars, rows, rows, rows, rows, here_k, here_v, there_k, there_v)


def scatter_sum(left, weight):
    n = weight.shape[1]
    split = n // 2
    first, second = weight[:, :split], weight[:, split:]
    depth = left.shape[-1]

    def times(rows, w):
        lead = rows.shape[:-1]
        return (
            jnp.dot(rows.reshape(-1, depth), w, preferred_element_type=jnp.float32)
            .astype(jnp.bfloat16)
            .reshape(lead + (w.shape[1],))
        )

    got_a = lax.ppermute(times(left[1], first), "exp", y_swap())
    got_b = [
        lax.ppermute(times(left[:, d], second), "exp", z_shift(d)) for d in (1, 3, 2)
    ]
    own_a = times(left[0], first)
    own_b = times(left[:, 0], second)
    sum_b = own_b.astype(jnp.float32) + sum(v.astype(jnp.float32) for v in got_b)
    later_b = lax.ppermute(sum_b[1].astype(jnp.bfloat16), "exp", y_swap())
    sum_a = own_a.astype(jnp.float32) + got_a.astype(jnp.float32)
    later_a = [
        lax.ppermute(sum_a[d].astype(jnp.bfloat16), "exp", z_shift(d)) for d in (1, 3, 2)
    ]
    return jnp.concatenate(
        [
            sum_a[0] + sum(v.astype(jnp.float32) for v in later_a),
            sum_b[0] + later_b.astype(jnp.float32),
        ],
        axis=1,
    )


def token_gather(own):
    half = own.shape[0] // 2
    a, b = own[:half], own[half:]
    a_near = [a] + [None] * 3
    for d in (1, 3, 2):
        a_near[d] = lax.ppermute(a, "exp", z_shift(-d))
    b_pair = jnp.stack([b, lax.ppermute(b, "exp", y_swap())])
    a_near = jnp.stack(a_near)
    a_far = lax.ppermute(a_near, "exp", y_swap())
    b_all = [b_pair] + [None] * 3
    for d in (1, 3, 2):
        b_all[d] = lax.ppermute(b_pair, "exp", z_shift(-d))
    return jnp.stack([jnp.stack([a_near, a_far]), jnp.stack(b_all, axis=1)])


def normalize(hidden):
    return (
        hidden * lax.rsqrt(jnp.mean(hidden * hidden, axis=-1, keepdims=True) + EPSILON)
    ).astype(jnp.bfloat16)


def shards(
    residual,
    mamba_input,
    mamba_gate,
    filter_taps,
    filter_bias,
    input_select,
    step_weight,
    step_bias,
    decay_log,
    skip_scale,
    output_weight,
    query_weight,
    key_matrix,
    value_matrix,
    head_weight,
    cache_keys,
    stored_cache_values,
    cache_state,
    cache_filter,
    prompt_slot,
    session_prompt,
):
    meta = jnp.stack([lax.axis_index("sess"), lax.axis_index("exp")]).astype(jnp.int32)
    scalars = (meta, session_prompt, prompt_slot)
    filter_here, filter_there = sess_gather(cache_filter)
    state_here, state_there = sess_gather(cache_state.astype(jnp.bfloat16))
    keys_here, keys_there = sess_gather(cache_keys)
    values_here, values_there = sess_gather(stored_cache_values)
    signal, part = conv_project(
        scalars, mamba_input, filter_here, filter_there, filter_taps, filter_bias, input_select
    )
    pieces = lax.all_to_all(part.reshape(8, OWN, -1), "exp", 0, 0, tiled=True)
    own = jnp.sum(pieces.astype(jnp.float32), axis=0).astype(jnp.bfloat16)
    projected = exp_gather(own)
    gated = scan_gate(
        scalars,
        projected,
        signal,
        mamba_gate,
        step_weight,
        step_bias,
        decay_log,
        state_here,
        state_there,
        skip_scale,
    )
    after_mamba = residual.astype(jnp.float32) + scatter_sum(gated, output_weight)
    tokens = token_gather(normalize(after_mamba))
    weight = jnp.concatenate([query_weight, key_matrix, value_matrix], axis=1)
    rows = (
        jnp.dot(
            tokens.reshape(-1, tokens.shape[-1]), weight, preferred_element_type=jnp.float32
        )
        .astype(jnp.bfloat16)
        .reshape(tokens.shape[:-1] + (weight.shape[1],))
    )
    heads_out = attend(scalars, rows, keys_here, values_here, keys_there, values_there)
    return (after_mamba + scatter_sum(heads_out, head_weight)).astype(jnp.bfloat16)


def solution(mesh):
    return jax.shard_map(
        shards,
        mesh=mesh,
        in_specs=(
            P(("sess", "exp"), None),
            P("sess", "exp"),
            P("sess", "exp"),
            P(None, "exp"),
            P("exp"),
            P("exp", None),
            P(None, "exp"),
            P("exp"),
            P(None, "exp"),
            P("exp"),
            P("exp", None),
            P(None, "exp"),
            P(None, "exp"),
            P(None, "exp"),
            P("exp", None),
            P("sess", None, "exp"),
            P("sess", None, "exp"),
            P("sess", None, "exp"),
            P("sess", None, "exp"),
            P(),
            P(),
        ),
        out_specs=P(("sess", "exp"), None),
        check_vma=False,
    )
```

```python
import functools
import math

import jax
import jax.numpy as jnp
from jax import lax
from jax.experimental import pallas as pl
from jax.experimental.pallas import tpu as pltpu
from jax.sharding import PartitionSpec as P

HEAD_SIZE = 128
NEW = 128
OWN = 64
EPSILON = 1e-06
LOG2E = math.log2(math.e)
MIB = 1 << 20


def y_swap():
    return [(y * 4 + z, (1 - y) * 4 + z) for y in range(2) for z in range(4)]


def z_shift(d):
    return [(y * 4 + z, y * 4 + (z + d) % 4) for y in range(2) for z in range(4)]


def sess_shift(far, x, core):
    return [
        (f * 8 + a * 2 + c, (f ^ far) * 8 + ((a + x) % 4) * 2 + (c ^ core))
        for f in range(2)
        for a in range(4)
        for c in range(2)
    ]


def from_y(value):
    half = value.shape[0] // 2
    direct, around = [], []
    for f in range(2):
        for low in range(8):
            for y in range(2):
                for z in range(4):
                    here = (f * 8 + low) * 8 + y * 4 + z
                    direct.append((here, (f * 8 + low) * 8 + (1 - y) * 4 + z))
                    around.append((here, ((1 - f) * 8 + low) * 8 + (1 - y) * 4 + z))
    return jnp.concatenate(
        [
            lax.ppermute(value[:half], ("sess", "exp"), direct),
            lax.ppermute(value[half:], ("sess", "exp"), around),
        ],
        axis=0,
    )


def copies_to_all(value, axis, count):
    return lax.all_to_all(
        jnp.broadcast_to(value[None], (count,) + value.shape), axis, 0, 0, tiled=True
    )


def session_of(g, meta):
    return ((meta[1] >> 2) ^ (g >> 1)) * 2 + (g & 1)


def slot_of(g, meta, prompts, slots):
    return slots[prompts[meta[0] * 4 + session_of(g, meta)]]


def place_of(g, meta, prompts, slots):
    slot = slot_of(g, meta, prompts, slots)
    holder = slot >> 1
    far = (holder >> 3) ^ (meta[0] >> 3)
    x = ((holder >> 1) - (meta[0] >> 1)) & 3
    return (x * 2 + far) * 2 + (slot & 1), (holder ^ meta[0]) & 1


def z_step(g, half, meta):
    return ((g & 1) * 2 + half - meta[1]) & 3


def cache_row_of(g, meta, prompts, slots):
    slot = slot_of(g, meta, prompts, slots)
    holder = slot >> 1
    far = (holder >> 3) ^ (meta[0] >> 3)
    return ((holder & 7) * 2 + far) * 2 + (slot & 1)


def row_of(g, meta, prompts, slots):
    return place_of(g, meta, prompts, slots)[0]


def side_of(g, meta, prompts, slots):
    return place_of(g, meta, prompts, slots)[1]


def conv_kernel(
    meta,
    prompts,
    slots,
    x_ref,
    prefix_ref,
    taps_ref,
    bias_ref,
    select_ref,
    out_ref,
    part_ref,
    series,
):
    new, channels = x_ref.shape
    rows = prefix_ref.shape[1]
    odd = (slot_of(pl.program_id(0), meta, prompts, slots) & 1) == 1
    for k in range(rows):
        pair = prefix_ref[0, k].astype(jnp.float32)
        series[8 - rows + k : 9 - rows + k] = jnp.where(odd, pair[1:2], pair[0:1])
    series[8:] = x_ref[...].astype(jnp.float32)
    total = jnp.broadcast_to(bias_ref[...], (new, channels))
    for k in range(taps_ref.shape[0]):
        total += taps_ref[k : k + 1] * series[8 - rows + k : 8 - rows + k + new]
    out = (total / (1.0 + jnp.exp(-total))).astype(jnp.bfloat16)
    out_ref[...] = out
    part_ref[...] = lax.dot_general(
        out, select_ref[...], (((1,), (1,)), ((), ())), preferred_element_type=jnp.float32
    ).astype(jnp.bfloat16)


def whole(a):
    return pl.BlockSpec(a.shape, lambda *_: (0,) * a.ndim)


def conv_project(scalars, x, prefixes, taps, bias, select):
    tokens, channels = x.shape
    width = select.shape[0]
    bias = bias.reshape(1, channels)

    def by_session(g, meta, prompts, slots):
        return session_of(g, meta), 0

    def by_holder(g, *refs):
        return slot_of(g, *refs) >> 1, 0, 0, 0

    return pl.pallas_call(
        conv_kernel,
        grid_spec=pltpu.PrefetchScalarGridSpec(
            num_scalar_prefetch=3,
            grid=(tokens // NEW,),
            in_specs=[
                pl.BlockSpec((NEW, channels), by_session),
                pl.BlockSpec((1,) + prefixes.shape[1:], by_holder),
                whole(taps),
                whole(bias),
                whole(select),
            ],
            out_specs=[
                pl.BlockSpec((NEW, channels), by_session),
                pl.BlockSpec((NEW, width), by_session),
            ],
            scratch_shapes=[pltpu.VMEM((NEW + 8, channels), jnp.float32)],
        ),
        out_shape=[
            jax.ShapeDtypeStruct((tokens, channels), jnp.bfloat16),
            jax.ShapeDtypeStruct((tokens, width), jnp.bfloat16),
        ],
        compiler_params=pltpu.CompilerParams(vmem_limit_bytes=60 * MIB),
        name="conv_project",
    )(*scalars, x, prefixes, taps, bias, select)


def scan_kernel(
    meta,
    prompts,
    slots,
    projected_ref,
    signal_ref,
    gate_ref,
    weight_ref,
    bias_ref,
    decay_ref,
    here_ref,
    there_ref,
    skip_ref,
    out_weight,
    part_a,
    part_b0,
    part_b1,
    part_b2,
    part_b3,
    rate_s,
    state_s,
    step_s,
    drive_s,
    emit_s,
    mix_s,
    gated_s,
    weight_s,
    sems,
    *,
    far,
):
    chunks = sems.shape[0]
    tile = out_weight.shape[1] // chunks

    def fetch(n):
        cols = pl.ds(n * tile, tile)
        return pltpu.make_async_copy(out_weight.at[:, cols], weight_s.at[:, cols], sems.at[n])

    g = pl.program_id(0) + 2 * far
    new, channels = signal_ref.shape
    states = decay_ref.shape[0]
    blocks = channels // 128
    rank = weight_ref.shape[0]
    half = new // 2

    @pl.when(pl.program_id(0) == 0)
    def _():
        for n in range(chunks):
            fetch(n).start()
        rate = jnp.exp(decay_ref[...]) * (-LOG2E)
        for b in range(blocks):
            rate_s[:, b, :] = rate[:, b * 128 : (b + 1) * 128]

    start = jnp.where(
        side_of(g, meta, prompts, slots) == 1,
        there_ref[0, :states].astype(jnp.float32),
        here_ref[0, :states].astype(jnp.float32),
    )
    for b in range(blocks):
        state_s[:, b, :] = start[:, b * 128 : (b + 1) * 128]
    projected = projected_ref[...]
    before = (
        jnp.dot(projected[:, :rank], weight_ref[...], preferred_element_type=jnp.float32)
        + bias_ref[...]
    )
    size = jnp.maximum(before, 0.0) + jnp.log1p(jnp.exp(-jnp.abs(before)))
    drive = size * signal_ref[...].astype(jnp.float32)
    for b in range(blocks):
        cols = slice(b * 128, (b + 1) * 128)
        step_s[:, b] = size[:, cols].reshape(new // 8, 8, 128)
        drive_s[:, b] = drive[:, cols].reshape(new // 8, 8, 128)
    mix = jnp.transpose(projected[:, rank:].astype(jnp.float32))
    for t in range(new):
        mix_s[t] = jnp.broadcast_to(mix[:, t : t + 1], (2 * states, 128))

    def advance(i, state):
        state = list(state)
        rates = [rate_s[n] for n in range(states)]
        for s in range(8):
            d = step_s[i, :, s, :]
            u = drive_s[i, :, s, :]
            t = i * 8 + s
            total = None
            for n in range(states):
                state[n] = jnp.exp2(d * rates[n]) * state[n] + u * mix_s[t, n : n + 1, :]
                term = state[n] * mix_s[t, states + n : states + n + 1, :]
                total = term if total is None else total + term
            emit_s[i, :, s, :] = total
        return tuple(state)

    lax.fori_loop(0, new // 8, advance, tuple(state_s[n] for n in range(states)))
    for b in range(blocks):
        cols = slice(b * 128, (b + 1) * 128)
        emitted = emit_s[:, b].reshape(new, 128)
        gate = gate_ref[:, cols].astype(jnp.float32)
        signal = signal_ref[:, cols].astype(jnp.float32)
        gated = (
            (emitted + skip_ref[:, cols] * signal) * (gate / (1.0 + jnp.exp(-gate)))
        ).astype(jnp.bfloat16)
        for k in range(2):
            gated_s[z_step(g, k, meta), :, cols] = gated[k * half : (k + 1) * half]

    @pl.when(pl.program_id(0) == pl.num_programs(0) - 1)
    def _():
        rows = gated_s[...].reshape(-1, channels)
        split = part_a.shape[-1]
        for n in range(chunks):
            fetch(n).wait()
            cols = slice(n * tile, (n + 1) * tile)
            out = jnp.dot(
                rows, weight_s[:, cols], preferred_element_type=jnp.float32
            ).astype(jnp.bfloat16)
            if n * tile < split:
                part_a[:, :, cols] = out.reshape(part_a.shape[0], half, tile)
            else:
                for d, ref in enumerate((part_b0, part_b1, part_b2, part_b3)):
                    ref[:, n * tile - split : (n + 1) * tile - split] = out[
                        d * half : (d + 1) * half
                    ]


def scan_gate(
    far, scalars, projected, signal, gate, weight, bias, decay, here, there, skip, out_weight
):
    tokens, channels = signal.shape
    states = decay.shape[0]
    blocks = channels // 128
    width = projected.shape[-1]
    features = out_weight.shape[1]
    split = features // 2
    bias = bias.reshape(1, channels)
    skip = skip.reshape(1, channels)

    def by_session(g, meta, prompts, slots):
        return session_of(g + 2 * far, meta), 0

    def by_row(g, *refs):
        return row_of(g + 2 * far, *refs), 0, 0

    return pl.pallas_call(
        functools.partial(scan_kernel, far=far),
        grid_spec=pltpu.PrefetchScalarGridSpec(
            num_scalar_prefetch=3,
            grid=(2,),
            in_specs=[
                pl.BlockSpec((NEW, width), by_session),
                pl.BlockSpec((NEW, channels), by_session),
                pl.BlockSpec((NEW, channels), by_session),
                whole(weight),
                whole(bias),
                whole(decay),
                pl.BlockSpec((1,) + here.shape[1:], by_row),
                pl.BlockSpec((1,) + here.shape[1:], by_row),
                whole(skip),
                pl.BlockSpec(memory_space=pltpu.HBM),
            ],
            out_specs=[pl.BlockSpec((4, OWN, split), lambda g, *_: (0, 0, 0))]
            + [pl.BlockSpec((OWN, features - split), lambda g, *_: (0, 0))] * 4,
            scratch_shapes=[
                pltpu.VMEM((states, blocks, 128), jnp.float32),
                pltpu.VMEM((states, blocks, 128), jnp.float32),
                pltpu.VMEM((NEW // 8, blocks, 8, 128), jnp.float32),
                pltpu.VMEM((NEW // 8, blocks, 8, 128), jnp.float32),
                pltpu.VMEM((NEW // 8, blocks, 8, 128), jnp.float32),
                pltpu.VMEM((NEW, 2 * states, 128), jnp.float32),
                pltpu.VMEM((4, OWN, channels), jnp.bfloat16),
                pltpu.VMEM((channels, features), jnp.bfloat16),
                pltpu.SemaphoreType.DMA((4,)),
            ],
        ),
        out_shape=[jax.ShapeDtypeStruct((4, OWN, split), jnp.bfloat16)]
        + [jax.ShapeDtypeStruct((OWN, features - split), jnp.bfloat16)] * 4,
        compiler_params=pltpu.CompilerParams(vmem_limit_bytes=60 * MIB),
        name="scan_far" if far else "scan_near",
    )(*scalars, projected, signal, gate, weight, bias, decay, here, there, skip, out_weight)


def pick_kernel(meta, prompts, slots, row_ref, out_ref):
    out_ref[...] = row_ref[...]


def pick_far(scalars, cached):
    shape = cached.shape[1:]
    return pl.pallas_call(
        pick_kernel,
        grid_spec=pltpu.PrefetchScalarGridSpec(
            num_scalar_prefetch=3,
            grid=(2,),
            in_specs=[
                pl.BlockSpec((1,) + shape, lambda g, *refs: (cache_row_of(g + 2, *refs), 0, 0))
            ],
            out_specs=pl.BlockSpec((1,) + shape, lambda g, *_: (g, 0, 0)),
        ),
        out_shape=jax.ShapeDtypeStruct((2,) + shape, cached.dtype),
        compiler_params=pltpu.CompilerParams(vmem_limit_bytes=60 * MIB),
        name="pick_far",
    )(*scalars, cached)


def serve_kernel(meta, prompts, slots, *refs):
    tokens, refs = refs[:8], refs[8:]
    (query, key, value, others, head, own_cache, far_cache), refs = refs[:7], refs[7:]
    outs, refs = refs[:4], refs[4:]
    (rows_s, weight_s, head_s, cache_s, total, heads_s, row_sem, weight_sem, cache_sem, head_sem) = refs
    features = rows_s.shape[1]
    side = features // 2
    depth = features // weight_sem.shape[0]
    lent = head.shape[0]
    widths = (query.shape[1], key.shape[1], value.shape[1])
    width = sum(widths)

    def token_copy(n):
        rows = pl.ds(n % 4 * OWN, OWN)
        return pltpu.make_async_copy(
            tokens[n], rows_s.at[rows, pl.ds(n // 4 * side, side)], row_sem.at[n]
        )

    def weight_copies(n):
        rows = pl.ds(n * depth, depth)
        copies, column = [], 0
        for k, (ref, size) in enumerate(zip((query, key, value), widths)):
            copies.append((ref.at[rows], column, size, k))
            column += size
        copies.append((others.at[rows, pl.ds(lent, width)], width, width, 3))
        return [
            pltpu.make_async_copy(
                source, weight_s.at[rows, pl.ds(at, size)], weight_sem.at[n, k]
            )
            for source, at, size, k in copies
        ]

    def cache_copies():
        return [
            pltpu.make_async_copy(
                own_cache.at[cache_row_of(g, meta, prompts, slots)], cache_s.at[0, g], cache_sem.at[0, g]
            )
            for g in range(2)
        ] + [
            pltpu.make_async_copy(far_cache.at[g], cache_s.at[1, g], cache_sem.at[1, g])
            for g in range(2)
        ]

    def head_copies(n):
        cols = pl.ds(n * lent, lent)
        return [
            pltpu.make_async_copy(head.at[:, cols], head_s.at[pl.ds(0, lent), cols], head_sem.at[0, n]),
            pltpu.make_async_copy(
                others.at[pl.ds(n * lent, lent), pl.ds(0, lent)],
                head_s.at[pl.ds(lent, lent), cols],
                head_sem.at[1, n],
            ),
        ]

    for n in range(8):
        token_copy(n).start()
    for n in range(features // depth):
        for copy in weight_copies(n):
            copy.start()
    for copy in cache_copies():
        copy.start()
    for n in range(features // lent):
        for copy in head_copies(n):
            copy.start()

    squares = None
    for n in range(features // depth):
        if n * depth % side == 0:
            for k in range(4):
                token_copy(n * depth // side * 4 + k).wait()
        for copy in weight_copies(n):
            copy.wait()
        rows = rows_s[:, n * depth : (n + 1) * depth]
        wide_rows = rows.astype(jnp.float32)
        wide_rows = wide_rows * wide_rows
        part = sum(wide_rows[:, b * 128 : (b + 1) * 128] for b in range(depth // 128))
        squares = part if squares is None else squares + part
        product = jnp.dot(
            rows, weight_s[n * depth : (n + 1) * depth], preferred_element_type=jnp.float32
        )
        if n == 0:
            total[...] = product
        else:
            total[...] += product
    scale = lax.rsqrt(jnp.sum(squares, axis=-1, keepdims=True) / features + EPSILON)

    for copy in cache_copies():
        copy.wait()
    new = 2 * OWN
    heads = widths[0] // HEAD_SIZE
    contract = (((1,), (1,)), ((), ()))
    shrink = 1.0 / math.sqrt(HEAD_SIZE)
    total[...] = total[...] * scale
    for g in range(2):
        steps = [pl.multiple_of(z_step(g, half, meta) * OWN, OWN) for half in range(2)]
        for side_of_y in range(2):
            cols = slice(side_of_y * width, (side_of_y + 1) * width)
            rows = jnp.concatenate(
                [total[pl.ds(at, OWN), cols] for at in steps], axis=0
            ).astype(jnp.bfloat16)
            old = cache_s[side_of_y, g]
            cached = old.shape[0] // 2
            old_keys, old_values = old[:cached], old[cached:]
            new_keys = rows[:, widths[0] : widths[0] + HEAD_SIZE]
            new_values = rows[:, widths[0] + HEAD_SIZE :]
            queries = jnp.concatenate(
                [rows[:, k * HEAD_SIZE : (k + 1) * HEAD_SIZE] for k in range(heads)], axis=0
            )
            before = (
                lax.dot_general(queries, old_keys, contract, preferred_element_type=jnp.float32)
                * shrink
            )
            fresh = (
                lax.dot_general(queries, new_keys, contract, preferred_element_type=jnp.float32)
                * shrink
            )
            at = lax.broadcasted_iota(jnp.int32, fresh.shape, 0) & (new - 1)
            fresh = jnp.where(lax.broadcasted_iota(jnp.int32, fresh.shape, 1) <= at, fresh, -1e30)
            top = jnp.maximum(
                jnp.max(before, axis=-1, keepdims=True), jnp.max(fresh, axis=-1, keepdims=True)
            )
            before = jnp.exp(before - top)
            fresh = jnp.exp(fresh - top)
            inverse = 1.0 / (
                jnp.sum(before, axis=-1, keepdims=True) + jnp.sum(fresh, axis=-1, keepdims=True)
            )
            attended = jnp.dot(
                (before * inverse).astype(jnp.bfloat16),
                old_values,
                preferred_element_type=jnp.float32,
            ) + jnp.dot(
                (fresh * inverse).astype(jnp.bfloat16),
                new_values,
                preferred_element_type=jnp.float32,
            )
            attended = attended.astype(jnp.bfloat16)
            for half in range(2):
                for k in range(heads):
                    column = side_of_y * widths[0] + k * HEAD_SIZE
                    heads_s[pl.ds(steps[half], OWN), column : column + HEAD_SIZE] = attended[
                        k * new + half * OWN : k * new + (half + 1) * OWN
                    ]

    for n in range(features // lent):
        for copy in head_copies(n):
            copy.wait()
        cols = slice(n * lent, (n + 1) * lent)
        out = jnp.dot(
            heads_s[...], head_s[:, cols], preferred_element_type=jnp.float32
        ).astype(jnp.bfloat16)
        for d, ref in enumerate(outs):
            ref[:, cols] = out[d * OWN : (d + 1) * OWN]


def serve(scalars, first, second, query, key, value, others, head, own_cache, far_cache):
    features = query.shape[0]
    width = query.shape[1] + key.shape[1] + value.shape[1]
    hbm = pl.BlockSpec(memory_space=pltpu.HBM)
    return pl.pallas_call(
        serve_kernel,
        grid_spec=pltpu.PrefetchScalarGridSpec(
            num_scalar_prefetch=3,
            grid=(1,),
            in_specs=[hbm] * 15,
            out_specs=[pl.BlockSpec((OWN, features), lambda *_: (0, 0))] * 4,
            scratch_shapes=[
                pltpu.VMEM((4 * OWN, features), jnp.bfloat16),
                pltpu.VMEM((features, 2 * width), jnp.bfloat16),
                pltpu.VMEM((2 * head.shape[0], features), jnp.bfloat16),
                pltpu.VMEM((2, 2) + own_cache.shape[1:], jnp.bfloat16),
                pltpu.VMEM((4 * OWN, 2 * width), jnp.float32),
                pltpu.VMEM((4 * OWN, 2 * query.shape[1]), jnp.bfloat16),
                pltpu.SemaphoreType.DMA((8,)),
                pltpu.SemaphoreType.DMA((4, 4)),
                pltpu.SemaphoreType.DMA((2, 2)),
                pltpu.SemaphoreType.DMA((2, features // head.shape[0])),
            ],
        ),
        out_shape=[jax.ShapeDtypeStruct((OWN, features), jnp.bfloat16)] * 4,
        compiler_params=pltpu.CompilerParams(vmem_limit_bytes=60 * MIB),
        name="serve",
    )(
        *scalars, *first, *second, query, key, value, others, head, own_cache, far_cache
    )


def after(value, *others):
    return lax.optimization_barrier((value,) + others)[0]


def wide(value):
    return value.astype(jnp.float32)


def send_far(part_a, *parts_b):
    got_b = [lax.ppermute(parts_b[d], "exp", z_shift(d)) for d in (1, 3, 2)]
    return lax.ppermute(part_a, "exp", y_swap()), parts_b[0], got_b


def finish(near, got_a, own_b, got_b):
    own_a, *parts_b = near
    near_b = [lax.ppermute(parts_b[d], "exp", z_shift(d)) for d in (1, 3, 2)]
    far_b = (wide(own_b) + sum(wide(v) for v in got_b)).astype(jnp.bfloat16)
    later_b = lax.ppermute(after(far_b, got_a), "exp", y_swap())
    sums_a = wide(own_a) + wide(got_a)
    rest_a = after(sums_a.astype(jnp.bfloat16), near_b[0], near_b[1], near_b[2])
    later_a = [lax.ppermute(rest_a[d], "exp", z_shift(d)) for d in (1, 3, 2)]
    sum_b = wide(parts_b[0]) + sum(wide(v) for v in near_b) + wide(later_b)
    sum_a = sums_a[0] + sum(wide(v) for v in later_a)
    return sum_a, sum_b


def z_gather(value):
    got = [value] + [None] * 3
    for d in (1, 3, 2):
        got[d] = lax.ppermute(value, "exp", z_shift(-d))
    return got


def shards(
    residual,
    mamba_input,
    mamba_gate,
    filter_taps,
    filter_bias,
    input_select,
    step_weight,
    step_bias,
    decay_log,
    skip_scale,
    output_weight,
    query_weight,
    key_matrix,
    value_matrix,
    head_weight,
    cache_keys,
    stored_cache_values,
    cache_state,
    cache_filter,
    prompt_slot,
    session_prompt,
):
    meta = jnp.stack([lax.axis_index("sess"), lax.axis_index("exp")]).astype(jnp.int32)
    scalars = (meta, session_prompt, prompt_slot)
    by_tap = jnp.swapaxes(cache_filter, 0, 1)
    copies = jnp.broadcast_to(by_tap[None], (16,) + by_tap.shape)
    prefixes = lax.all_to_all(copies, "sess", 0, 0, tiled=True)
    start = after(cache_state.astype(jnp.bfloat16), prefixes)
    start_far = lax.ppermute(start, "sess", sess_shift(1, 0, 0))
    groups = [list(range(8)), list(range(8, 16))]
    cached = jnp.concatenate([cache_keys, stored_cache_values], axis=1)
    cached = after(cached, prefixes)
    cached_far = lax.ppermute(cached, "sess", sess_shift(1, 0, 0))
    signal, part = conv_project(
        scalars,
        mamba_input,
        prefixes,
        filter_taps,
        filter_bias,
        input_select.T,
    )
    start_pair = jnp.concatenate(
        [start, after(start_far, part)], axis=0
    )
    start_here = jnp.concatenate(
        [start_pair] + [lax.ppermute(start_pair, "sess", sess_shift(0, -d, 0)) for d in (1, 2, 3)],
        axis=0,
    )
    start_there = lax.ppermute(start_here, "sess", sess_shift(0, 0, 1))
    cached = lax.all_gather(
        jnp.concatenate([cached, after(cached_far, part)], axis=0),
        "sess",
        axis=0,
        tiled=True,
        axis_index_groups=groups,
    )
    pieces = lax.all_to_all(part.reshape(8, OWN, -1), "exp", 0, 0, tiled=True)
    own = jnp.sum(wide(pieces), axis=0).astype(jnp.bfloat16)
    projected = copies_to_all(own, "exp", 8).reshape(8 * OWN, -1)
    eighth = lax.axis_index("sess") % 8
    share = query_weight.shape[0] // 8
    lent = jnp.concatenate(
        [lax.dynamic_slice_in_dim(head_weight, eighth * share, share, 1)]
        + [
            lax.dynamic_slice_in_dim(w, eighth * share, share, 0)
            for w in (query_weight, key_matrix, value_matrix)
        ],
        axis=1,
    )
    lent = from_y(after(lent, projected))

    def scan(far, projected):
        return scan_gate(
            far,
            scalars,
            projected,
            signal,
            mamba_gate,
            step_weight,
            step_bias,
            decay_log,
            start_here,
            start_there,
            skip_scale,
            output_weight,
        )

    far = scan(1, projected)
    others = lax.all_gather(
        after(lent, cached, far[0]), "sess", axis=0, tiled=True, axis_index_groups=groups
    )
    sent = send_far(*far)
    near = scan(0, after(projected, *far))
    sum_a, sum_b = finish(near, *sent)
    split = residual.shape[1] // 2
    after_a = wide(residual[:, :split]) + sum_a
    after_b = wide(residual[:, split:]) + sum_b
    far_cache = lax.ppermute(after(pick_far(scalars, cached), sum_b), "exp", y_swap())
    tokens_b = z_gather(after_b.astype(jnp.bfloat16))
    tokens_a = z_gather(after_a.astype(jnp.bfloat16))
    products = serve(
        scalars,
        tokens_a,
        tokens_b,
        query_weight,
        key_matrix,
        value_matrix,
        others,
        head_weight,
        cached,
        far_cache,
    )
    got = [lax.ppermute(products[d], "exp", z_shift(d)) for d in (1, 3, 2)]
    head_total = sum(wide(v) for v in [products[0]] + got)
    return (jnp.concatenate([after_a, after_b], axis=1) + head_total).astype(jnp.bfloat16)


def solution(mesh):
    return jax.shard_map(
        shards,
        mesh=mesh,
        in_specs=(
            P(("sess", "exp"), None),
            P("sess", "exp"),
            P("sess", "exp"),
            P(None, "exp"),
            P("exp"),
            P("exp", None),
            P(None, "exp"),
            P("exp"),
            P(None, "exp"),
            P("exp"),
            P("exp", None),
            P(None, "exp"),
            P(None, "exp"),
            P(None, "exp"),
            P("exp", None),
            P("sess", None, "exp"),
            P("sess", None, "exp"),
            P("sess", None, "exp"),
            P("sess", None, "exp"),
            P(),
            P(),
        ),
        out_specs=P(("sess", "exp"), None),
        check_vma=False,
    )
```

```python
import functools
import math

import jax
import jax.numpy as jnp
from jax import lax
from jax.experimental import pallas as pl
from jax.experimental.pallas import tpu as pltpu
from jax.sharding import PartitionSpec as P

HEAD_SIZE = 128
NEW = 128
OWN = 64
EPSILON = 1e-06
LOG2E = math.log2(math.e)
MIB = 1 << 20


def y_swap():
    return [(y * 4 + z, (1 - y) * 4 + z) for y in range(2) for z in range(4)]


def z_shift(d):
    return [(y * 4 + z, y * 4 + (z + d) % 4) for y in range(2) for z in range(4)]


def sess_shift(far, x, core):
    return [
        (f * 8 + a * 2 + c, (f ^ far) * 8 + ((a + x) % 4) * 2 + (c ^ core))
        for f in range(2)
        for a in range(4)
        for c in range(2)
    ]


def around():
    return [
        ((f * 8 + low) * 8 + y * 4 + z, ((1 - f) * 8 + low) * 8 + (1 - y) * 4 + z)
        for f in range(2)
        for low in range(8)
        for y in range(2)
        for z in range(4)
    ]


def copies_to_all(value, axis, count):
    return lax.all_to_all(
        jnp.broadcast_to(value[None], (count,) + value.shape), axis, 0, 0, tiled=True
    )


def session_of(g, meta):
    return ((meta[1] >> 2) ^ (g >> 1)) * 2 + (g & 1)


def slot_of(g, meta, prompts, slots):
    return slots[prompts[meta[0] * 4 + session_of(g, meta)]]


def place_of(g, meta, prompts, slots):
    slot = slot_of(g, meta, prompts, slots)
    holder = slot >> 1
    far = (holder >> 3) ^ (meta[0] >> 3)
    x = ((holder >> 1) - (meta[0] >> 1)) & 3
    return (x * 2 + far) * 2 + (slot & 1), (holder ^ meta[0]) & 1


def z_step(g, half, meta):
    return ((g & 1) * 2 + half - meta[1]) & 3


def cache_row_of(g, meta, prompts, slots):
    slot = slot_of(g, meta, prompts, slots)
    holder = slot >> 1
    far = (holder >> 3) ^ (meta[0] >> 3)
    return ((holder & 7) * 2 + far) * 2 + (slot & 1)


def row_of(g, meta, prompts, slots):
    return place_of(g, meta, prompts, slots)[0]


def side_of(g, meta, prompts, slots):
    return place_of(g, meta, prompts, slots)[1]


def in_smem():
    return pl.BlockSpec(memory_space=pltpu.SMEM)


def in_vmem():
    return pl.BlockSpec(memory_space=pltpu.VMEM)


def silu(value):
    return 0.5 * value * (1.0 + jnp.tanh(0.5 * value))


def in_any():
    return pl.BlockSpec(memory_space=pl.ANY)


def filtered(series, taps, bias, first, count):
    total = jnp.broadcast_to(bias, (count, series.shape[1]))
    for k in range(taps.shape[0]):
        total += taps[k : k + 1] * series[first + k : first + k + count]
    return silu(total).astype(jnp.bfloat16)


def times_select(out, select):
    return lax.dot_general(
        out, select, (((1,), (1,)), ((), ())), preferred_element_type=jnp.float32
    ).astype(jnp.bfloat16)


def conv_kernel(
    x_any, taps_any, bias_any, select_any, out_ref, part_ref, series, x_s, taps_s, bias_s, select_s, sems
):
    sessions = x_s.shape[0]
    shared = [
        pltpu.make_async_copy(source, target, sems.at[n])
        for n, (source, target) in enumerate(
            ((taps_any, taps_s), (bias_any, bias_s), (select_any, select_s))
        )
    ]
    own = [
        pltpu.make_async_copy(x_any.at[pl.ds(g * NEW, NEW)], x_s.at[g], sems.at[3 + g])
        for g in range(sessions)
    ]
    for copy in shared + own:
        copy.start()
    series[:8] = jnp.zeros((8, series.shape[1]), jnp.float32)
    for copy in shared:
        copy.wait()
    for g in range(sessions):
        at = slice(g * NEW, (g + 1) * NEW)
        own[g].wait()
        series[8:] = x_s[g].astype(jnp.float32)
        out = filtered(series, taps_s, bias_s[...], 9 - taps_s.shape[0], NEW)
        out_ref[at] = out
        part_ref[at] = times_select(out, select_s[...])


def conv_project(x, taps, bias, select):
    tokens, channels = x.shape
    sessions = tokens // NEW
    return pl.pallas_call(
        conv_kernel,
        in_specs=[in_any()] * 4,
        out_specs=[in_vmem()] * 2,
        out_shape=[
            jax.ShapeDtypeStruct((tokens, channels), jnp.bfloat16),
            jax.ShapeDtypeStruct((tokens, select.shape[0]), jnp.bfloat16),
        ],
        scratch_shapes=[
            pltpu.VMEM((NEW + 8, channels), jnp.float32),
            pltpu.VMEM((sessions, NEW, channels), jnp.bfloat16),
            pltpu.VMEM(taps.shape, jnp.float32),
            pltpu.VMEM((1, channels), jnp.float32),
            pltpu.VMEM(select.shape, jnp.bfloat16),
            pltpu.SemaphoreType.DMA((3 + sessions,)),
        ],
        compiler_params=pltpu.CompilerParams(vmem_limit_bytes=56 * MIB),
        cost_estimate=pl.CostEstimate(flops=4 * 10**9, bytes_accessed=16 * MIB, transcendentals=0),
        name="conv_project",
    )(x, taps, bias.reshape(1, channels), select)


def head_rows_kernel(
    meta,
    prompts,
    slots,
    x_any,
    prefix_any,
    taps_any,
    bias_any,
    select_any,
    signal_ref,
    products_ref,
    out_ref,
    part_ref,
    series,
    x_s,
    prefix_s,
    taps_s,
    bias_s,
    select_s,
    sems,
):
    sessions, count = x_s.shape[:2]
    rows = prefix_s.shape[1]

    def slot(g):
        return slot_of(g, meta, prompts, slots)

    def place(g):
        return pl.ds(pl.multiple_of(session_of(g, meta) * NEW, NEW), count)

    copies = [
        pltpu.make_async_copy(source, target, sems.at[n])
        for n, (source, target) in enumerate(
            ((taps_any, taps_s), (bias_any, bias_s), (select_any, select_s))
        )
    ]
    for g in range(sessions):
        copies += [
            pltpu.make_async_copy(prefix_any.at[slot(g) >> 1], prefix_s.at[g], sems.at[3 + 2 * g]),
            pltpu.make_async_copy(x_any.at[place(g)], x_s.at[g], sems.at[4 + 2 * g]),
        ]
    for copy in copies:
        copy.start()
    out_ref[...] = signal_ref[...]
    part_ref[...] = products_ref[...]
    for copy in copies:
        copy.wait()
    outs = []
    for g in range(sessions):
        odd = (slot(g) & 1) == 1
        for k in range(rows):
            pair = prefix_s[g, k].astype(jnp.float32)
            series[8 - rows + k : 9 - rows + k] = jnp.where(odd, pair[1:2], pair[0:1])
        series[8:] = x_s[g].astype(jnp.float32)
        outs.append(filtered(series, taps_s, bias_s[...], 8 - rows, count))
    products = times_select(jnp.concatenate(outs, axis=0), select_s[...])
    for g in range(sessions):
        out_ref[place(g)] = outs[g]
        part_ref[place(g)] = products[g * count : (g + 1) * count]


def head_rows(scalars, x, prefixes, taps, bias, select, signal, products):
    tokens, channels = x.shape
    sessions = tokens // NEW
    return pl.pallas_call(
        head_rows_kernel,
        in_specs=[in_smem()] * 3 + [in_any()] * 5 + [in_vmem()] * 2,
        out_specs=[in_vmem()] * 2,
        out_shape=[
            jax.ShapeDtypeStruct(signal.shape, signal.dtype),
            jax.ShapeDtypeStruct(products.shape, products.dtype),
        ],
        scratch_shapes=[
            pltpu.VMEM((16 + 8, channels), jnp.float32),
            pltpu.VMEM((sessions, 16, channels), jnp.bfloat16),
            pltpu.VMEM((sessions,) + prefixes.shape[1:], jnp.bfloat16),
            pltpu.VMEM(taps.shape, jnp.float32),
            pltpu.VMEM((1, channels), jnp.float32),
            pltpu.VMEM(select.shape, jnp.bfloat16),
            pltpu.SemaphoreType.DMA((3 + 2 * sessions,)),
        ],
        compiler_params=pltpu.CompilerParams(vmem_limit_bytes=56 * MIB),
        name="head_rows",
    )(*scalars, x, prefixes, taps, bias.reshape(1, channels), select, signal, products)


def scan_kernel(
    meta,
    prompts,
    slots,
    projected_ref,
    signal_ref,
    gate_ref,
    weight_ref,
    bias_ref,
    decay_ref,
    here_ref,
    there_ref,
    skip_ref,
    out_weight_any,
    part_a,
    part_b0,
    part_b1,
    part_b2,
    part_b3,
    rate_s,
    state_s,
    step_s,
    drive_s,
    emit_s,
    mix_s,
    gated_s,
    out_weight,
    sems,
    *,
    far,
):
    channels = signal_ref.shape[1]
    tile = 1024
    def out_copy(n):
        cols = pl.ds(n * tile, tile)
        return pltpu.make_async_copy(
            out_weight_any.at[:, cols], out_weight.at[:, cols], sems.at[n]
        )

    states = decay_ref.shape[0]
    blocks = channels // 128
    rank = weight_ref.shape[0]
    new = NEW
    half = OWN

    rate = jnp.exp(decay_ref[...]) * (-LOG2E)
    for b in range(blocks):
        rate_s[:, b, :] = rate[:, b * 128 : (b + 1) * 128]

    for i in range(2):
        g = 2 * far + i
        if i == 1:
            for n in range(out_weight.shape[1] // tile):
                out_copy(n).start()
        at = pl.ds(pl.multiple_of(session_of(g, meta) * new, new), new)
        row = row_of(g, meta, prompts, slots)
        start = jnp.where(
            side_of(g, meta, prompts, slots) == 1,
            there_ref[row, :states].astype(jnp.float32),
            here_ref[row, :states].astype(jnp.float32),
        )
        for b in range(blocks):
            state_s[:, b, :] = start[:, b * 128 : (b + 1) * 128]
        projected = projected_ref[at]
        before = (
            jnp.dot(projected[:, :rank], weight_ref[...], preferred_element_type=jnp.float32)
            + bias_ref[...]
        )
        size = jnp.maximum(before, 0.0) + jnp.log1p(jnp.exp(-jnp.abs(before)))
        drive = size * signal_ref[at].astype(jnp.float32)
        for b in range(blocks):
            cols = slice(b * 128, (b + 1) * 128)
            step_s[:, b] = size[:, cols].reshape(new // 8, 8, 128)
            drive_s[:, b] = drive[:, cols].reshape(new // 8, 8, 128)
        mix = jnp.transpose(projected[:, rank:].astype(jnp.float32))
        for t in range(new):
            mix_s[t] = jnp.broadcast_to(mix[:, t : t + 1], (2 * states, 128))

        def advance(block, state):
            state = list(state)
            rates = [rate_s[n] for n in range(states)]
            for s in range(8):
                d = step_s[block, :, s, :]
                u = drive_s[block, :, s, :]
                t = block * 8 + s
                total = None
                for n in range(states):
                    state[n] = jnp.exp2(d * rates[n]) * state[n] + u * mix_s[t, n : n + 1, :]
                    term = state[n] * mix_s[t, states + n : states + n + 1, :]
                    total = term if total is None else total + term
                emit_s[block, :, s, :] = total
            return tuple(state)

        lax.fori_loop(
            0, new // 8, advance, tuple(state_s[n] for n in range(states)), unroll=2
        )
        for b in range(blocks):
            cols = slice(b * 128, (b + 1) * 128)
            emitted = emit_s[:, b].reshape(new, 128)
            gate = gate_ref[at, cols].astype(jnp.float32)
            signal = signal_ref[at, cols].astype(jnp.float32)
            gated = ((emitted + skip_ref[:, cols] * signal) * silu(gate)).astype(jnp.bfloat16)
            for k in range(2):
                gated_s[z_step(g, k, meta), :, cols] = gated[k * half : (k + 1) * half]

    rows = gated_s[...].reshape(-1, channels)
    split = part_a.shape[-1]
    for n in range(out_weight.shape[1] // tile):
        out_copy(n).wait()
        cols = slice(n * tile, (n + 1) * tile)
        out = jnp.dot(
            rows, out_weight[:, cols], preferred_element_type=jnp.float32
        ).astype(jnp.bfloat16)
        if n * tile < split:
            part_a[:, :, cols] = out.reshape(part_a.shape[0], half, tile)
        else:
            for d, ref in enumerate((part_b0, part_b1, part_b2, part_b3)):
                ref[:, n * tile - split : (n + 1) * tile - split] = out[d * half : (d + 1) * half]


def scan_gate(
    far, scalars, projected, signal, gate, weight, bias, decay, here, there, skip, out_weight
):
    channels = signal.shape[1]
    states = decay.shape[0]
    blocks = channels // 128
    features = out_weight.shape[1]
    split = features // 2
    return pl.pallas_call(
        functools.partial(scan_kernel, far=far),
        in_specs=[in_smem()] * 3 + [in_vmem()] * 9 + [in_any()],
        out_specs=[in_vmem()] * 5,
        out_shape=[jax.ShapeDtypeStruct((4, OWN, split), jnp.bfloat16)]
        + [jax.ShapeDtypeStruct((OWN, features - split), jnp.bfloat16)] * 4,
        scratch_shapes=[
            pltpu.VMEM((states, blocks, 128), jnp.float32),
            pltpu.VMEM((states, blocks, 128), jnp.float32),
            pltpu.VMEM((NEW // 8, blocks, 8, 128), jnp.float32),
            pltpu.VMEM((NEW // 8, blocks, 8, 128), jnp.float32),
            pltpu.VMEM((NEW // 8, blocks, 8, 128), jnp.float32),
            pltpu.VMEM((NEW, 2 * states, 128), jnp.float32),
            pltpu.VMEM((4, OWN, channels), jnp.bfloat16),
            pltpu.VMEM(out_weight.shape, jnp.bfloat16),
            pltpu.SemaphoreType.DMA((features // 1024,)),
        ],
        compiler_params=pltpu.CompilerParams(vmem_limit_bytes=50 * MIB),
        name="scan_far" if far else "scan_near",
    )(
        *scalars,
        projected,
        signal,
        gate,
        weight,
        bias.reshape(1, channels),
        decay,
        here,
        there,
        skip.reshape(1, channels),
        out_weight,
    )


def pick_kernel(meta, prompts, slots, row_ref, out_ref):
    out_ref[...] = row_ref[...]


def pick_far(scalars, cached):
    shape = cached.shape[1:]
    return pl.pallas_call(
        pick_kernel,
        grid_spec=pltpu.PrefetchScalarGridSpec(
            num_scalar_prefetch=3,
            grid=(2,),
            in_specs=[
                pl.BlockSpec((1,) + shape, lambda g, *refs: (cache_row_of(g + 2, *refs), 0, 0))
            ],
            out_specs=pl.BlockSpec((1,) + shape, lambda g, *_: (g, 0, 0)),
        ),
        out_shape=jax.ShapeDtypeStruct((2,) + shape, cached.dtype),
        compiler_params=pltpu.CompilerParams(vmem_limit_bytes=58 * MIB),
        name="pick_far",
    )(*scalars, cached)


def serve_kernel(meta, prompts, slots, *refs):
    tokens, refs = refs[:8], refs[8:]
    (query, key, value, others, head, far_cache, own_cache), refs = refs[:7], refs[7:]
    outs, refs = refs[:4], refs[4:]
    rows_s, weight_s, total, heads_s, cache_s, head_s, row_sem, weight_sem, cache_sem, head_sem = refs
    features = query.shape[0]
    side = features // 2
    lent = head.shape[0]
    widths = (query.shape[1], key.shape[1], value.shape[1])
    width = sum(widths)
    pieces = weight_sem.shape[0]
    depth = features // pieces

    token_copies = [
        pltpu.make_async_copy(
            ref, rows_s.at[pl.ds(n % 4 * OWN, OWN), pl.ds(n // 4 * side, side)], row_sem.at[n]
        )
        for n, ref in enumerate(tokens)
    ]

    def weight_copies(n):
        rows = pl.ds(n * depth, depth)
        copies, column = [], 0
        for k, ref in enumerate((query, key, value, others)):
            skip = lent if k == 3 else 0
            size = ref.shape[1] - skip
            copies.append(
                pltpu.make_async_copy(
                    ref.at[rows, pl.ds(skip, size)],
                    weight_s.at[rows, pl.ds(column, size)],
                    weight_sem.at[n, k],
                )
            )
            column += size
        return copies

    cache_copies = [
        pltpu.make_async_copy(
            own_cache.at[cache_row_of(g, meta, prompts, slots)], cache_s.at[0, g], cache_sem.at[0, g]
        )
        for g in range(2)
    ] + [
        pltpu.make_async_copy(far_cache.at[g], cache_s.at[1, g], cache_sem.at[1, g])
        for g in range(2)
    ]

    def head_copies(n):
        cols = pl.ds(n * lent, lent)
        return [
            pltpu.make_async_copy(
                head.at[:, cols], head_s.at[pl.ds(0, lent), cols], head_sem.at[0, n]
            ),
            pltpu.make_async_copy(
                others.at[cols, pl.ds(0, lent)], head_s.at[pl.ds(lent, lent), cols], head_sem.at[1, n]
            ),
        ]

    def begin(copies):
        for copy in copies:
            copy.start()

    blocks = features // lent
    begin(token_copies)
    begin(weight_copies(0))
    begin(weight_copies(1))
    squares = 0.0
    for n in range(pieces):
        if n * depth % side == 0:
            for copy in token_copies[n * depth // side * 4 :][:4]:
                copy.wait()
        for copy in weight_copies(n):
            copy.wait()
        if n + 2 < pieces:
            begin(weight_copies(n + 2))
        elif n + 2 == pieces:
            begin(cache_copies)
            for m in range(blocks // 2):
                begin(head_copies(m))
        else:
            for m in range(blocks // 2, blocks):
                begin(head_copies(m))
        deep = slice(n * depth, (n + 1) * depth)
        rows = rows_s[:, deep]
        wide_rows = rows.astype(jnp.float32)
        wide_rows = wide_rows * wide_rows
        squares += sum(wide_rows[:, b * 128 : (b + 1) * 128] for b in range(depth // 128))
        product = jnp.dot(rows, weight_s[deep], preferred_element_type=jnp.float32)
        if n == 0:
            total[...] = product
        else:
            total[...] += product
    scale = lax.rsqrt(jnp.sum(squares, axis=-1, keepdims=True) / features + EPSILON)
    total[...] = total[...] * scale
    for copy in cache_copies:
        copy.wait()
    new = 2 * OWN
    heads = widths[0] // HEAD_SIZE
    contract = (((1,), (1,)), ((), ()))
    shrink = LOG2E / math.sqrt(HEAD_SIZE)
    for g in range(2):
        steps = [pl.multiple_of(z_step(g, half, meta) * OWN, OWN) for half in range(2)]
        for side_of_y in range(2):
            cols = slice(side_of_y * width, (side_of_y + 1) * width)
            rows = jnp.concatenate(
                [total[pl.ds(at, OWN), cols] for at in steps], axis=0
            ).astype(jnp.bfloat16)
            old = cache_s[side_of_y, g]
            cached = old.shape[0] // 2
            old_keys, old_values = old[:cached], old[cached:]
            new_keys = rows[:, widths[0] : widths[0] + HEAD_SIZE]
            new_values = rows[:, widths[0] + HEAD_SIZE :]
            queries = jnp.concatenate(
                [rows[:, k * HEAD_SIZE : (k + 1) * HEAD_SIZE] for k in range(heads)], axis=0
            )
            before = lax.dot_general(
                queries, old_keys, contract, preferred_element_type=jnp.float32
            )
            fresh = lax.dot_general(queries, new_keys, contract, preferred_element_type=jnp.float32)
            at = lax.broadcasted_iota(jnp.int32, fresh.shape, 0) & (new - 1)
            fresh = jnp.where(lax.broadcasted_iota(jnp.int32, fresh.shape, 1) <= at, fresh, -1e30)
            top = shrink * jnp.maximum(
                jnp.max(before, axis=-1, keepdims=True), jnp.max(fresh, axis=-1, keepdims=True)
            )
            before = jnp.exp2(before * shrink - top).astype(jnp.bfloat16)
            fresh = jnp.exp2(fresh * shrink - top).astype(jnp.bfloat16)
            ones = jnp.ones((cached, HEAD_SIZE), jnp.bfloat16)
            attended = jnp.dot(
                before,
                jnp.concatenate([old_values, ones], axis=1),
                preferred_element_type=jnp.float32,
            ) + jnp.dot(
                fresh,
                jnp.concatenate([new_values, ones[:new]], axis=1),
                preferred_element_type=jnp.float32,
            )
            attended = (attended[:, :HEAD_SIZE] / attended[:, HEAD_SIZE:]).astype(jnp.bfloat16)
            for half in range(2):
                for k in range(heads):
                    column = side_of_y * widths[0] + k * HEAD_SIZE
                    heads_s[pl.ds(steps[half], OWN), column : column + HEAD_SIZE] = attended[
                        k * new + half * OWN : k * new + (half + 1) * OWN
                    ]

    for n in range(blocks):
        for copy in head_copies(n):
            copy.wait()
        cols = slice(n * lent, (n + 1) * lent)
        out = jnp.dot(
            heads_s[...], head_s[:, cols], preferred_element_type=jnp.float32
        ).astype(jnp.bfloat16)
        for d, ref in enumerate(outs):
            ref[:, cols] = out[d * OWN : (d + 1) * OWN]


def serve(scalars, first, second, query, key, value, others, head, own_cache, far_cache):
    features = query.shape[0]
    width = query.shape[1] + key.shape[1] + value.shape[1]
    return pl.pallas_call(
        serve_kernel,
        in_specs=[in_smem()] * 3 + [in_any()] * 15,
        out_specs=[in_vmem()] * 4,
        out_shape=[jax.ShapeDtypeStruct((OWN, features), jnp.bfloat16)] * 4,
        scratch_shapes=[
            pltpu.VMEM((4 * OWN, features), jnp.bfloat16),
            pltpu.VMEM((features, 2 * width), jnp.bfloat16),
            pltpu.VMEM((4 * OWN, 2 * width), jnp.float32),
            pltpu.VMEM((4 * OWN, 2 * query.shape[1]), jnp.bfloat16),
            pltpu.VMEM((2, 2) + own_cache.shape[1:], jnp.bfloat16),
            pltpu.VMEM((2 * head.shape[0], features), jnp.bfloat16),
            pltpu.SemaphoreType.DMA((8,)),
            pltpu.SemaphoreType.DMA((8, 4)),
            pltpu.SemaphoreType.DMA((2, 2)),
            pltpu.SemaphoreType.DMA((2, features // head.shape[0])),
        ],
        compiler_params=pltpu.CompilerParams(vmem_limit_bytes=56 * MIB),
        name="serve",
    )(*scalars, *first, *second, query, key, value, others, head, far_cache, own_cache)


def after(value, *others):
    return lax.optimization_barrier((value,) + others)[0]


def wide(value):
    return value.astype(jnp.float32)


def send_far(part_a, *parts_b):
    got_b = [lax.ppermute(parts_b[d], "exp", z_shift(d)) for d in (1, 3, 2)]
    return lax.ppermute(part_a, "exp", y_swap()), parts_b[0], got_b


def finish(near, got_a, own_b, got_b):
    own_a, *parts_b = near
    near_b = [lax.ppermute(parts_b[d], "exp", z_shift(d)) for d in (1, 3, 2)]
    far_b = (wide(own_b) + sum(wide(v) for v in got_b)).astype(jnp.bfloat16)
    later_b = lax.ppermute(after(far_b, got_a), "exp", y_swap())
    sums_a = wide(own_a) + wide(got_a)
    rest_a = after(sums_a.astype(jnp.bfloat16), near_b[0], near_b[1], near_b[2])
    later_a = [lax.ppermute(rest_a[d], "exp", z_shift(d)) for d in (1, 3, 2)]
    sum_b = wide(parts_b[0]) + sum(wide(v) for v in near_b) + wide(later_b)
    sum_a = sums_a[0] + sum(wide(v) for v in later_a)
    return sum_a, sum_b


def z_gather(value):
    got = [value] + [None] * 3
    for d in (1, 3, 2):
        got[d] = lax.ppermute(value, "exp", z_shift(-d))
    return got


def shards(
    residual,
    mamba_input,
    mamba_gate,
    filter_taps,
    filter_bias,
    input_select,
    step_weight,
    step_bias,
    decay_log,
    skip_scale,
    output_weight,
    query_weight,
    key_matrix,
    value_matrix,
    head_weight,
    cache_keys,
    stored_cache_values,
    cache_state,
    cache_filter,
    prompt_slot,
    session_prompt,
):
    meta = jnp.stack([lax.axis_index("sess"), lax.axis_index("exp")]).astype(jnp.int32)
    scalars = (meta, session_prompt, prompt_slot)
    by_tap = jnp.swapaxes(cache_filter, 0, 1)
    copies = jnp.broadcast_to(by_tap[None], (16,) + by_tap.shape)
    prefixes = lax.all_to_all(copies, "sess", 0, 0, tiled=True)
    start = after(cache_state.astype(jnp.bfloat16), copies)
    start_far = lax.ppermute(start, "sess", sess_shift(1, 0, 0))
    start_pair = jnp.concatenate([start, start_far], axis=0)
    start_x = [lax.ppermute(start_pair, "sess", sess_shift(0, -d, 0)) for d in (1, 2, 3)]
    signal, part = conv_project(after(mamba_input, start_pair), filter_taps, filter_bias, input_select.T)
    cached = jnp.concatenate([cache_keys, stored_cache_values], axis=1)
    cached = after(cached, start_far)
    cached_far = lax.ppermute(cached, "sess", sess_shift(1, 0, 0))
    signal, part = head_rows(
        scalars,
        mamba_input,
        prefixes,
        filter_taps,
        filter_bias,
        input_select.T,
        signal,
        part,
    )
    part = after(part, *start_x)
    start_here = jnp.concatenate([start_pair] + start_x, axis=0)
    start_there = lax.ppermute(start_here, "sess", sess_shift(0, 0, 1))
    pieces = lax.all_to_all(part.reshape(8, OWN, -1), "exp", 0, 0, tiled=True)
    own = jnp.sum(wide(pieces), axis=0).astype(jnp.bfloat16)
    projected = copies_to_all(own, "exp", 8).reshape(8 * OWN, -1)
    groups = [list(range(8)), list(range(8, 16))]
    cached = lax.all_gather(
        jnp.concatenate([cached, after(cached_far, part)], axis=0),
        "sess",
        axis=0,
        tiled=True,
        axis_index_groups=groups,
    )
    eighth = lax.axis_index("sess") % 8
    share = query_weight.shape[0] // 8
    lent = jnp.concatenate(
        [lax.dynamic_slice_in_dim(head_weight, eighth * share, share, 1)]
        + [
            lax.dynamic_slice_in_dim(w, eighth * share, share, 0)
            for w in (query_weight, key_matrix, value_matrix)
        ],
        axis=1,
    )
    lent = lax.ppermute(after(lent, own), ("sess", "exp"), around())

    def scan(far, projected):
        return scan_gate(
            far,
            scalars,
            projected,
            signal,
            mamba_gate,
            step_weight,
            step_bias,
            decay_log,
            start_here,
            start_there,
            skip_scale,
            output_weight,
        )

    far = scan(1, projected)
    def scan(far, projected):
        return scan_gate(
            far,
            scalars,
            projected,
            signal,
            mamba_gate,
            step_weight,
            step_bias,
            decay_log,
            start_here,
            start_there,
            skip_scale,
            output_weight,
        )

    far = scan(1, projected)
    others = lax.all_gather(
        after(lent, cached, projected), "sess", axis=0, tiled=True, axis_index_groups=groups
    )

    others = lax.all_gather(
        after(lent, far[0]), "sess", axis=0, tiled=True, axis_index_groups=groups
    )
    sent = send_far(*far)
    near = scan(0, after(projected, *far))
    sum_a, sum_b = finish(near, *sent)
    split = residual.shape[1] // 2
    after_a = wide(residual[:, :split]) + sum_a
    after_b = wide(residual[:, split:]) + sum_b
    far_cache = lax.ppermute(after(pick_far(scalars, cached), sum_b), "exp", y_swap())
    tokens_b = z_gather(after_b.astype(jnp.bfloat16))
    tokens_a = z_gather(after_a.astype(jnp.bfloat16))
    products = serve(
        scalars,
        tokens_a,
        tokens_b,
        query_weight,
        key_matrix,
        value_matrix,
        others,
        head_weight,
        cached,
        far_cache,
    )
    got = [lax.ppermute(products[d], "exp", z_shift(d)) for d in (1, 3, 2)]
    head_total = sum(wide(v) for v in [products[0]] + got)
    return (jnp.concatenate([after_a, after_b], axis=1) + head_total).astype(jnp.bfloat16)


def solution(mesh):
    return jax.shard_map(
        shards,
        mesh=mesh,
        in_specs=(
            P(("sess", "exp"), None),
            P("sess", "exp"),
            P("sess", "exp"),
            P(None, "exp"),
            P("exp"),
            P("exp", None),
            P(None, "exp"),
            P("exp"),
            P(None, "exp"),
            P("exp"),
            P("exp", None),
            P(None, "exp"),
            P(None, "exp"),
            P(None, "exp"),
            P("exp", None),
            P("sess", None, "exp"),
            P("sess", None, "exp"),
            P("sess", None, "exp"),
            P("sess", None, "exp"),
            P(),
            P(),
        ),
        out_specs=P(("sess", "exp"), None),
        check_vma=False,
    )
```

```python
import functools
import math

import jax
import jax.numpy as jnp
from jax import lax
from jax.experimental import pallas as pl
from jax.experimental.pallas import tpu as pltpu
from jax.sharding import PartitionSpec as P

HEAD_SIZE = 128
NEW = 128
OWN = 64
EPSILON = 1e-06
LOG2E = math.log2(math.e)
MIB = 1 << 20


def y_swap():
    return [(y * 4 + z, (1 - y) * 4 + z) for y in range(2) for z in range(4)]


def z_shift(d):
    return [(y * 4 + z, y * 4 + (z + d) % 4) for y in range(2) for z in range(4)]


def sess_shift(far, x, core):
    return [
        (f * 8 + a * 2 + c, (f ^ far) * 8 + ((a + x) % 4) * 2 + (c ^ core))
        for f in range(2)
        for a in range(4)
        for c in range(2)
    ]


def around():
    return [
        ((f * 8 + low) * 8 + y * 4 + z, ((1 - f) * 8 + low) * 8 + (1 - y) * 4 + z)
        for f in range(2)
        for low in range(8)
        for y in range(2)
        for z in range(4)
    ]


def copies_to_all(value, axis, count):
    return lax.all_to_all(
        jnp.broadcast_to(value[None], (count,) + value.shape), axis, 0, 0, tiled=True
    )


def session_of(g, meta):
    return ((meta[1] >> 2) ^ (g >> 1)) * 2 + (g & 1)


def slot_of(g, meta, prompts, slots):
    return slots[prompts[meta[0] * 4 + session_of(g, meta)]]


def place_of(g, meta, prompts, slots):
    slot = slot_of(g, meta, prompts, slots)
    holder = slot >> 1
    far = (holder >> 3) ^ (meta[0] >> 3)
    x = ((holder >> 1) - (meta[0] >> 1)) & 3
    return (x * 2 + far) * 2 + (slot & 1), (holder ^ meta[0]) & 1


def z_step(g, half, meta):
    return ((g & 1) * 2 + half - meta[1]) & 3


def cache_row_of(g, meta, prompts, slots):
    slot = slot_of(g, meta, prompts, slots)
    holder = slot >> 1
    far = (holder >> 3) ^ (meta[0] >> 3)
    return ((holder & 7) * 2 + far) * 2 + (slot & 1)


def row_of(g, meta, prompts, slots):
    return place_of(g, meta, prompts, slots)[0]


def side_of(g, meta, prompts, slots):
    return place_of(g, meta, prompts, slots)[1]


def in_smem():
    return pl.BlockSpec(memory_space=pltpu.SMEM)


def in_vmem():
    return pl.BlockSpec(memory_space=pltpu.VMEM)


def silu(value):
    return 0.5 * value * (1.0 + jnp.tanh(0.5 * value))


def in_any():
    return pl.BlockSpec(memory_space=pl.ANY)


def filtered(series, taps, bias, first, count):
    total = jnp.broadcast_to(bias, (count, series.shape[1]))
    for k in range(taps.shape[0]):
        total += taps[k : k + 1] * series[first + k : first + k + count]
    return silu(total).astype(jnp.bfloat16)


def times_select(out, select):
    return lax.dot_general(
        out, select, (((1,), (1,)), ((), ())), preferred_element_type=jnp.float32
    ).astype(jnp.bfloat16)


def conv_kernel(
    x_any, taps_any, bias_any, select_any, out_ref, part_ref, series, x_s, taps_s, bias_s, select_s, sems
):
    sessions = x_s.shape[0]
    shared = [
        pltpu.make_async_copy(source, target, sems.at[n])
        for n, (source, target) in enumerate(
            ((taps_any, taps_s), (bias_any, bias_s), (select_any, select_s))
        )
    ]
    own = [
        pltpu.make_async_copy(x_any.at[pl.ds(g * NEW, NEW)], x_s.at[g], sems.at[3 + g])
        for g in range(sessions)
    ]
    for copy in shared + own:
        copy.start()
    series[:8] = jnp.zeros((8, series.shape[1]), jnp.float32)
    for copy in shared:
        copy.wait()
    for g in range(sessions):
        at = slice(g * NEW, (g + 1) * NEW)
        own[g].wait()
        series[8:] = x_s[g].astype(jnp.float32)
        out = filtered(series, taps_s, bias_s[...], 9 - taps_s.shape[0], NEW)
        out_ref[at] = out
        part_ref[at] = times_select(out, select_s[...])


def conv_project(x, taps, bias, select):
    tokens, channels = x.shape
    sessions = tokens // NEW
    return pl.pallas_call(
        conv_kernel,
        in_specs=[in_any()] * 4,
        out_specs=[in_vmem()] * 2,
        out_shape=[
            jax.ShapeDtypeStruct((tokens, channels), jnp.bfloat16),
            jax.ShapeDtypeStruct((tokens, select.shape[0]), jnp.bfloat16),
        ],
        scratch_shapes=[
            pltpu.VMEM((NEW + 8, channels), jnp.float32),
            pltpu.VMEM((sessions, NEW, channels), jnp.bfloat16),
            pltpu.VMEM(taps.shape, jnp.float32),
            pltpu.VMEM((1, channels), jnp.float32),
            pltpu.VMEM(select.shape, jnp.bfloat16),
            pltpu.SemaphoreType.DMA((3 + sessions,)),
        ],
        compiler_params=pltpu.CompilerParams(vmem_limit_bytes=56 * MIB),
        cost_estimate=pl.CostEstimate(flops=4 * 10**9, bytes_accessed=16 * MIB, transcendentals=0),
        name="conv_project",
    )(x, taps, bias.reshape(1, channels), select)


def head_rows_kernel(
    meta,
    prompts,
    slots,
    x_any,
    prefix_any,
    taps_any,
    bias_any,
    select_any,
    signal_ref,
    products_ref,
    out_ref,
    part_ref,
    series,
    x_s,
    prefix_s,
    taps_s,
    bias_s,
    select_s,
    sems,
):
    sessions, count = x_s.shape[:2]
    rows = prefix_s.shape[1]

    def slot(g):
        return slot_of(g, meta, prompts, slots)

    def place(g):
        return pl.ds(pl.multiple_of(session_of(g, meta) * NEW, NEW), count)

    copies = [
        pltpu.make_async_copy(source, target, sems.at[n])
        for n, (source, target) in enumerate(
            ((taps_any, taps_s), (bias_any, bias_s), (select_any, select_s))
        )
    ]
    for g in range(sessions):
        copies += [
            pltpu.make_async_copy(prefix_any.at[slot(g) >> 1], prefix_s.at[g], sems.at[3 + 2 * g]),
            pltpu.make_async_copy(x_any.at[place(g)], x_s.at[g], sems.at[4 + 2 * g]),
        ]
    for copy in copies:
        copy.start()
    out_ref[...] = signal_ref[...]
    part_ref[...] = products_ref[...]
    for copy in copies:
        copy.wait()
    outs = []
    for g in range(sessions):
        odd = (slot(g) & 1) == 1
        for k in range(rows):
            pair = prefix_s[g, k].astype(jnp.float32)
            series[8 - rows + k : 9 - rows + k] = jnp.where(odd, pair[1:2], pair[0:1])
        series[8:] = x_s[g].astype(jnp.float32)
        outs.append(filtered(series, taps_s, bias_s[...], 8 - rows, count))
    products = times_select(jnp.concatenate(outs, axis=0), select_s[...])
    for g in range(sessions):
        out_ref[place(g)] = outs[g]
        part_ref[place(g)] = products[g * count : (g + 1) * count]


def head_rows(scalars, x, prefixes, taps, bias, select, signal, products):
    tokens, channels = x.shape
    sessions = tokens // NEW
    return pl.pallas_call(
        head_rows_kernel,
        in_specs=[in_smem()] * 3 + [in_any()] * 5 + [in_vmem()] * 2,
        out_specs=[in_vmem()] * 2,
        out_shape=[
            jax.ShapeDtypeStruct(signal.shape, signal.dtype),
            jax.ShapeDtypeStruct(products.shape, products.dtype),
        ],
        scratch_shapes=[
            pltpu.VMEM((16 + 8, channels), jnp.float32),
            pltpu.VMEM((sessions, 16, channels), jnp.bfloat16),
            pltpu.VMEM((sessions,) + prefixes.shape[1:], jnp.bfloat16),
            pltpu.VMEM(taps.shape, jnp.float32),
            pltpu.VMEM((1, channels), jnp.float32),
            pltpu.VMEM(select.shape, jnp.bfloat16),
            pltpu.SemaphoreType.DMA((3 + 2 * sessions,)),
        ],
        compiler_params=pltpu.CompilerParams(vmem_limit_bytes=56 * MIB),
        name="head_rows",
    )(*scalars, x, prefixes, taps, bias.reshape(1, channels), select, signal, products)


def scan_kernel(
    meta,
    prompts,
    slots,
    projected_ref,
    signal_ref,
    gate_ref,
    weight_ref,
    bias_ref,
    decay_ref,
    here_ref,
    there_ref,
    skip_ref,
    out_weight_any,
    part_a,
    part_b0,
    part_b1,
    part_b2,
    part_b3,
    rate_s,
    state_s,
    step_s,
    drive_s,
    emit_s,
    mix_s,
    gated_s,
    out_weight,
    sems,
    *,
    far,
):
    channels = signal_ref.shape[1]
    tile = 1024
    def out_copy(n):
        cols = pl.ds(n * tile, tile)
        return pltpu.make_async_copy(
            out_weight_any.at[:, cols], out_weight.at[:, cols], sems.at[n]
        )

    states = decay_ref.shape[0]
    blocks = channels // 128
    rank = weight_ref.shape[0]
    new = NEW
    half = OWN

    rate = jnp.exp(decay_ref[...]) * (-LOG2E)
    for b in range(blocks):
        rate_s[:, b, :] = rate[:, b * 128 : (b + 1) * 128]

    for i in range(2):
        g = 2 * far + i
        if i == 1:
            for n in range(out_weight.shape[1] // tile):
                out_copy(n).start()
        at = pl.ds(pl.multiple_of(session_of(g, meta) * new, new), new)
        row = row_of(g, meta, prompts, slots)
        start = jnp.where(
            side_of(g, meta, prompts, slots) == 1,
            there_ref[row, :states].astype(jnp.float32),
            here_ref[row, :states].astype(jnp.float32),
        )
        for b in range(blocks):
            state_s[:, b, :] = start[:, b * 128 : (b + 1) * 128]
        projected = projected_ref[at]
        before = (
            jnp.dot(projected[:, :rank], weight_ref[...], preferred_element_type=jnp.float32)
            + bias_ref[...]
        )
        size = jnp.maximum(before, 0.0) + jnp.log1p(jnp.exp(-jnp.abs(before)))
        drive = size * signal_ref[at].astype(jnp.float32)
        for b in range(blocks):
            cols = slice(b * 128, (b + 1) * 128)
            step_s[:, b] = size[:, cols].reshape(new // 8, 8, 128)
            drive_s[:, b] = drive[:, cols].reshape(new // 8, 8, 128)
        mix = jnp.transpose(projected[:, rank:].astype(jnp.float32))
        for t in range(new):
            mix_s[t] = jnp.broadcast_to(mix[:, t : t + 1], (2 * states, 128))

        def advance(block, state):
            state = list(state)
            rates = [rate_s[n] for n in range(states)]
            for s in range(8):
                d = step_s[block, :, s, :]
                u = drive_s[block, :, s, :]
                t = block * 8 + s
                total = None
                for n in range(states):
                    state[n] = jnp.exp2(d * rates[n]) * state[n] + u * mix_s[t, n : n + 1, :]
                    term = state[n] * mix_s[t, states + n : states + n + 1, :]
                    total = term if total is None else total + term
                emit_s[block, :, s, :] = total
            return tuple(state)

        lax.fori_loop(
            0, new // 8, advance, tuple(state_s[n] for n in range(states)), unroll=2
        )
        for b in range(blocks):
            cols = slice(b * 128, (b + 1) * 128)
            emitted = emit_s[:, b].reshape(new, 128)
            gate = gate_ref[at, cols].astype(jnp.float32)
            signal = signal_ref[at, cols].astype(jnp.float32)
            gated = ((emitted + skip_ref[:, cols] * signal) * silu(gate)).astype(jnp.bfloat16)
            for k in range(2):
                gated_s[z_step(g, k, meta), :, cols] = gated[k * half : (k + 1) * half]

    rows = gated_s[...].reshape(-1, channels)
    split = part_a.shape[-1]
    for n in range(out_weight.shape[1] // tile):
        out_copy(n).wait()
        cols = slice(n * tile, (n + 1) * tile)
        out = jnp.dot(
            rows, out_weight[:, cols], preferred_element_type=jnp.float32
        ).astype(jnp.bfloat16)
        if n * tile < split:
            part_a[:, :, cols] = out.reshape(part_a.shape[0], half, tile)
        else:
            for d, ref in enumerate((part_b0, part_b1, part_b2, part_b3)):
                ref[:, n * tile - split : (n + 1) * tile - split] = out[d * half : (d + 1) * half]


def scan_gate(
    far, scalars, projected, signal, gate, weight, bias, decay, here, there, skip, out_weight
):
    channels = signal.shape[1]
    states = decay.shape[0]
    blocks = channels // 128
    features = out_weight.shape[1]
    split = features // 2
    return pl.pallas_call(
        functools.partial(scan_kernel, far=far),
        in_specs=[in_smem()] * 3 + [in_vmem()] * 9 + [in_any()],
        out_specs=[in_vmem()] * 5,
        out_shape=[jax.ShapeDtypeStruct((4, OWN, split), jnp.bfloat16)]
        + [jax.ShapeDtypeStruct((OWN, features - split), jnp.bfloat16)] * 4,
        scratch_shapes=[
            pltpu.VMEM((states, blocks, 128), jnp.float32),
            pltpu.VMEM((states, blocks, 128), jnp.float32),
            pltpu.VMEM((NEW // 8, blocks, 8, 128), jnp.float32),
            pltpu.VMEM((NEW // 8, blocks, 8, 128), jnp.float32),
            pltpu.VMEM((NEW // 8, blocks, 8, 128), jnp.float32),
            pltpu.VMEM((NEW, 2 * states, 128), jnp.float32),
            pltpu.VMEM((4, OWN, channels), jnp.bfloat16),
            pltpu.VMEM(out_weight.shape, jnp.bfloat16),
            pltpu.SemaphoreType.DMA((features // 1024,)),
        ],
        compiler_params=pltpu.CompilerParams(vmem_limit_bytes=50 * MIB),
        name="scan_far" if far else "scan_near",
    )(
        *scalars,
        projected,
        signal,
        gate,
        weight,
        bias.reshape(1, channels),
        decay,
        here,
        there,
        skip.reshape(1, channels),
        out_weight,
    )


def pick_kernel(meta, prompts, slots, row_ref, out_ref):
    out_ref[...] = row_ref[...]


def pick_far(scalars, cached):
    shape = cached.shape[1:]
    return pl.pallas_call(
        pick_kernel,
        grid_spec=pltpu.PrefetchScalarGridSpec(
            num_scalar_prefetch=3,
            grid=(2,),
            in_specs=[
                pl.BlockSpec((1,) + shape, lambda g, *refs: (cache_row_of(g + 2, *refs), 0, 0))
            ],
            out_specs=pl.BlockSpec((1,) + shape, lambda g, *_: (g, 0, 0)),
        ),
        out_shape=jax.ShapeDtypeStruct((2,) + shape, cached.dtype),
        compiler_params=pltpu.CompilerParams(vmem_limit_bytes=58 * MIB),
        name="pick_far",
    )(*scalars, cached)


def serve_kernel(meta, prompts, slots, *refs):
    tokens, refs = refs[:8], refs[8:]
    (query, key, value, others, head, far_cache, own_cache), refs = refs[:7], refs[7:]
    outs, refs = refs[:4], refs[4:]
    rows_s, weight_s, total, heads_s, cache_s, head_s, row_sem, weight_sem, cache_sem, head_sem = refs
    features = query.shape[0]
    side = features // 2
    lent = head.shape[0]
    widths = (query.shape[1], key.shape[1], value.shape[1])
    width = sum(widths)
    pieces = weight_sem.shape[0]
    depth = features // pieces

    token_copies = [
        pltpu.make_async_copy(
            ref, rows_s.at[pl.ds(n % 4 * OWN, OWN), pl.ds(n // 4 * side, side)], row_sem.at[n]
        )
        for n, ref in enumerate(tokens)
    ]

    def weight_copies(n):
        rows = pl.ds(n * depth, depth)
        copies, column = [], 0
        for k, ref in enumerate((query, key, value, others)):
            skip = lent if k == 3 else 0
            size = ref.shape[1] - skip
            copies.append(
                pltpu.make_async_copy(
                    ref.at[rows, pl.ds(skip, size)],
                    weight_s.at[rows, pl.ds(column, size)],
                    weight_sem.at[n, k],
                )
            )
            column += size
        return copies

    cache_copies = [
        pltpu.make_async_copy(
            own_cache.at[cache_row_of(g, meta, prompts, slots)], cache_s.at[0, g], cache_sem.at[0, g]
        )
        for g in range(2)
    ] + [
        pltpu.make_async_copy(far_cache.at[g], cache_s.at[1, g], cache_sem.at[1, g])
        for g in range(2)
    ]

    def head_copies(n):
        cols = pl.ds(n * lent, lent)
        return [
            pltpu.make_async_copy(
                head.at[:, cols], head_s.at[pl.ds(0, lent), cols], head_sem.at[0, n]
            ),
            pltpu.make_async_copy(
                others.at[cols, pl.ds(0, lent)], head_s.at[pl.ds(lent, lent), cols], head_sem.at[1, n]
            ),
        ]

    def begin(copies):
        for copy in copies:
            copy.start()

    blocks = features // lent
    begin(token_copies)
    begin(weight_copies(0))
    begin(weight_copies(1))
    squares = 0.0
    for n in range(pieces):
        if n * depth % side == 0:
            for copy in token_copies[n * depth // side * 4 :][:4]:
                copy.wait()
        for copy in weight_copies(n):
            copy.wait()
        if n + 2 < pieces:
            begin(weight_copies(n + 2))
        elif n + 2 == pieces:
            begin(cache_copies)
            for m in range(blocks // 2):
                begin(head_copies(m))
        else:
            for m in range(blocks // 2, blocks):
                begin(head_copies(m))
        deep = slice(n * depth, (n + 1) * depth)
        rows = rows_s[:, deep]
        wide_rows = rows.astype(jnp.float32)
        wide_rows = wide_rows * wide_rows
        squares += sum(wide_rows[:, b * 128 : (b + 1) * 128] for b in range(depth // 128))
        product = jnp.dot(rows, weight_s[deep], preferred_element_type=jnp.float32)
        if n == 0:
            total[...] = product
        else:
            total[...] += product
    scale = lax.rsqrt(jnp.sum(squares, axis=-1, keepdims=True) / features + EPSILON)
    total[...] = total[...] * scale
    for copy in cache_copies:
        copy.wait()
    new = 2 * OWN
    heads = widths[0] // HEAD_SIZE
    contract = (((1,), (1,)), ((), ()))
    shrink = LOG2E / math.sqrt(HEAD_SIZE)
    for g in range(2):
        steps = [pl.multiple_of(z_step(g, half, meta) * OWN, OWN) for half in range(2)]
        for side_of_y in range(2):
            cols = slice(side_of_y * width, (side_of_y + 1) * width)
            rows = jnp.concatenate(
                [total[pl.ds(at, OWN), cols] for at in steps], axis=0
            ).astype(jnp.bfloat16)
            old = cache_s[side_of_y, g]
            cached = old.shape[0] // 2
            old_keys, old_values = old[:cached], old[cached:]
            new_keys = rows[:, widths[0] : widths[0] + HEAD_SIZE]
            new_values = rows[:, widths[0] + HEAD_SIZE :]
            queries = jnp.concatenate(
                [rows[:, k * HEAD_SIZE : (k + 1) * HEAD_SIZE] for k in range(heads)], axis=0
            )
            before = lax.dot_general(
                queries, old_keys, contract, preferred_element_type=jnp.float32
            )
            fresh = lax.dot_general(queries, new_keys, contract, preferred_element_type=jnp.float32)
            at = lax.broadcasted_iota(jnp.int32, fresh.shape, 0) & (new - 1)
            fresh = jnp.where(lax.broadcasted_iota(jnp.int32, fresh.shape, 1) <= at, fresh, -1e30)
            top = shrink * jnp.maximum(
                jnp.max(before, axis=-1, keepdims=True), jnp.max(fresh, axis=-1, keepdims=True)
            )
            before = jnp.exp2(before * shrink - top).astype(jnp.bfloat16)
            fresh = jnp.exp2(fresh * shrink - top).astype(jnp.bfloat16)
            ones = jnp.ones((cached, HEAD_SIZE), jnp.bfloat16)
            attended = jnp.dot(
                before,
                jnp.concatenate([old_values, ones], axis=1),
                preferred_element_type=jnp.float32,
            ) + jnp.dot(
                fresh,
                jnp.concatenate([new_values, ones[:new]], axis=1),
                preferred_element_type=jnp.float32,
            )
            attended = (attended[:, :HEAD_SIZE] / attended[:, HEAD_SIZE:]).astype(jnp.bfloat16)
            for half in range(2):
                for k in range(heads):
                    column = side_of_y * widths[0] + k * HEAD_SIZE
                    heads_s[pl.ds(steps[half], OWN), column : column + HEAD_SIZE] = attended[
                        k * new + half * OWN : k * new + (half + 1) * OWN
                    ]

    for n in range(blocks):
        for copy in head_copies(n):
            copy.wait()
    for n in range(blocks):
        cols = slice(n * lent, (n + 1) * lent)
        out = jnp.dot(
            heads_s[...], head_s[:, cols], preferred_element_type=jnp.float32
        ).astype(jnp.bfloat16)
        for d, ref in enumerate(outs):
            ref[:, cols] = out[d * OWN : (d + 1) * OWN]


def serve(scalars, first, second, query, key, value, others, head, own_cache, far_cache):
    features = query.shape[0]
    width = query.shape[1] + key.shape[1] + value.shape[1]
    return pl.pallas_call(
        serve_kernel,
        in_specs=[in_smem()] * 3 + [in_any()] * 15,
        out_specs=[in_vmem()] * 4,
        out_shape=[jax.ShapeDtypeStruct((OWN, features), jnp.bfloat16)] * 4,
        scratch_shapes=[
            pltpu.VMEM((4 * OWN, features), jnp.bfloat16),
            pltpu.VMEM((features, 2 * width), jnp.bfloat16),
            pltpu.VMEM((4 * OWN, 2 * width), jnp.float32),
            pltpu.VMEM((4 * OWN, 2 * query.shape[1]), jnp.bfloat16),
            pltpu.VMEM((2, 2) + own_cache.shape[1:], jnp.bfloat16),
            pltpu.VMEM((2 * head.shape[0], features), jnp.bfloat16),
            pltpu.SemaphoreType.DMA((8,)),
            pltpu.SemaphoreType.DMA((4, 4)),
            pltpu.SemaphoreType.DMA((2, 2)),
            pltpu.SemaphoreType.DMA((2, features // head.shape[0])),
        ],
        compiler_params=pltpu.CompilerParams(vmem_limit_bytes=56 * MIB),
        name="serve",
    )(*scalars, *first, *second, query, key, value, others, head, far_cache, own_cache)


def after(value, *others):
    return lax.optimization_barrier((value,) + others)[0]


def wide(value):
    return value.astype(jnp.float32)


def send_far(part_a, *parts_b):
    got_b = [lax.ppermute(parts_b[d], "exp", z_shift(d)) for d in (1, 3, 2)]
    return lax.ppermute(part_a, "exp", y_swap()), parts_b[0], got_b


def finish(near, got_a, own_b, got_b):
    own_a, *parts_b = near
    near_b = [lax.ppermute(parts_b[d], "exp", z_shift(d)) for d in (1, 3, 2)]
    far_b = (wide(own_b) + sum(wide(v) for v in got_b)).astype(jnp.bfloat16)
    later_b = lax.ppermute(after(far_b, got_a), "exp", y_swap())
    sums_a = wide(own_a) + wide(got_a)
    rest_a = after(sums_a.astype(jnp.bfloat16), near_b[0], near_b[1], near_b[2])
    later_a = [lax.ppermute(rest_a[d], "exp", z_shift(d)) for d in (1, 3, 2)]
    sum_b = wide(parts_b[0]) + sum(wide(v) for v in near_b) + wide(later_b)
    sum_a = sums_a[0] + sum(wide(v) for v in later_a)
    return sum_a, sum_b


def z_gather(value):
    got = [value] + [None] * 3
    for d in (1, 3, 2):
        got[d] = lax.ppermute(value, "exp", z_shift(-d))
    return got


def shards(
    residual,
    mamba_input,
    mamba_gate,
    filter_taps,
    filter_bias,
    input_select,
    step_weight,
    step_bias,
    decay_log,
    skip_scale,
    output_weight,
    query_weight,
    key_matrix,
    value_matrix,
    head_weight,
    cache_keys,
    stored_cache_values,
    cache_state,
    cache_filter,
    prompt_slot,
    session_prompt,
):
    meta = jnp.stack([lax.axis_index("sess"), lax.axis_index("exp")]).astype(jnp.int32)
    scalars = (meta, session_prompt, prompt_slot)
    by_tap = jnp.swapaxes(cache_filter, 0, 1)
    copies = jnp.broadcast_to(by_tap[None], (16,) + by_tap.shape)
    prefixes = lax.all_to_all(copies, "sess", 0, 0, tiled=True)
    start = after(cache_state.astype(jnp.bfloat16), copies)
    start_far = lax.ppermute(start, "sess", sess_shift(1, 0, 0))
    start_pair = jnp.concatenate([start, start_far], axis=0)
    start_x = [lax.ppermute(start_pair, "sess", sess_shift(0, -d, 0)) for d in (1, 2, 3)]
    signal, part = conv_project(after(mamba_input, start_pair), filter_taps, filter_bias, input_select.T)
    cached = jnp.concatenate([cache_keys, stored_cache_values], axis=1)
    cached = after(cached, start_far)
    cached_far = lax.ppermute(cached, "sess", sess_shift(1, 0, 0))
    signal, part = head_rows(
        scalars,
        mamba_input,
        prefixes,
        filter_taps,
        filter_bias,
        input_select.T,
        signal,
        part,
    )
    part = after(part, *start_x)
    start_here = jnp.concatenate([start_pair] + start_x, axis=0)
    start_there = lax.ppermute(start_here, "sess", sess_shift(0, 0, 1))
    pieces = lax.all_to_all(part.reshape(8, OWN, -1), "exp", 0, 0, tiled=True)
    own = jnp.sum(wide(pieces), axis=0).astype(jnp.bfloat16)
    projected = copies_to_all(own, "exp", 8).reshape(8 * OWN, -1)
    groups = [list(range(8)), list(range(8, 16))]
    cached = lax.all_gather(
        jnp.concatenate([cached, after(cached_far, part)], axis=0),
        "sess",
        axis=0,
        tiled=True,
        axis_index_groups=groups,
    )
    eighth = lax.axis_index("sess") % 8
    share = query_weight.shape[0] // 8
    lent = jnp.concatenate(
        [lax.dynamic_slice_in_dim(head_weight, eighth * share, share, 1)]
        + [
            lax.dynamic_slice_in_dim(w, eighth * share, share, 0)
            for w in (query_weight, key_matrix, value_matrix)
        ],
        axis=1,
    )
    lent = lax.ppermute(after(lent, own), ("sess", "exp"), around())

    def scan(far, projected):
        return scan_gate(
            far,
            scalars,
            projected,
            signal,
            mamba_gate,
            step_weight,
            step_bias,
            decay_log,
            start_here,
            start_there,
            skip_scale,
            output_weight,
        )

    far = scan(1, projected)
    def scan(far, projected):
        return scan_gate(
            far,
            scalars,
            projected,
            signal,
            mamba_gate,
            step_weight,
            step_bias,
            decay_log,
            start_here,
            start_there,
            skip_scale,
            output_weight,
        )

    far = scan(1, projected)
    others = lax.all_gather(
        after(lent, cached, projected), "sess", axis=0, tiled=True, axis_index_groups=groups
    )

    others = lax.all_gather(
        after(lent, far[0]), "sess", axis=0, tiled=True, axis_index_groups=groups
    )
    sent = send_far(*far)
    near = scan(0, after(projected, *far))
    sum_a, sum_b = finish(near, *sent)
    split = residual.shape[1] // 2
    after_a = wide(residual[:, :split]) + sum_a
    after_b = wide(residual[:, split:]) + sum_b
    far_cache = lax.ppermute(after(pick_far(scalars, cached), sum_b), "exp", y_swap())
    tokens_b = z_gather(after_b.astype(jnp.bfloat16))
    tokens_a = z_gather(after_a.astype(jnp.bfloat16))
    products = serve(
        scalars,
        tokens_a,
        tokens_b,
        query_weight,
        key_matrix,
        value_matrix,
        others,
        head_weight,
        cached,
        far_cache,
    )
    got = [lax.ppermute(products[d], "exp", z_shift(d)) for d in (1, 3, 2)]
    head_total = sum(wide(v) for v in [products[0]] + got)
    return (jnp.concatenate([after_a, after_b], axis=1) + head_total).astype(jnp.bfloat16)


def solution(mesh):
    return jax.shard_map(
        shards,
        mesh=mesh,
        in_specs=(
            P(("sess", "exp"), None),
            P("sess", "exp"),
            P("sess", "exp"),
            P(None, "exp"),
            P("exp"),
            P("exp", None),
            P(None, "exp"),
            P("exp"),
            P(None, "exp"),
            P("exp"),
            P("exp", None),
            P(None, "exp"),
            P(None, "exp"),
            P(None, "exp"),
            P("exp", None),
            P("sess", None, "exp"),
            P("sess", None, "exp"),
            P("sess", None, "exp"),
            P("sess", None, "exp"),
            P(),
            P(),
        ),
        out_specs=P(("sess", "exp"), None),
        check_vma=False,
    )
```
